32 devices in a mesh: section: 4 (over x, core), seq: 8 (over z, y).
Axes of the slice: x: 2, y: 2, z: 4, core: 2. Of those that a mesh axis runs over, the one named last changes fastest.
Arguments:
- saved_section_input: bfloat16 [4, 1024, 1024], P('section', 'seq'), may hold values from -6 to 6
- out_cot: bfloat16 [4, 1024, 1024], P('section', 'seq'), may hold values from -6 to 6
- kernel_weight: bfloat16 [4, 2, 3, 64, 16, 32], P('section'), may hold values from -0.875 to 0.875
- blend_weight: bfloat16 [4, 2, 1024, 1024], P('section'), may hold values from -0.1875 to 0.1875
- hazard_head: bfloat16 [1024, 64], replicated, may hold values from -0.75 to 0.75
- labels: int32 [1024], P('seq'), may hold values from 0 to 63
- events: int32 [1024], P('seq'), may hold values 0 or 1
Outputs:
- input_grad: bfloat16 [4, 1024, 1024], P('section', 'seq')
- next_cot: bfloat16 [4, 1024, 1024], P('section', 'seq')
- mix_grad: float32 [4, 1024, 2, 1024], P('section', 'seq')
- conv_grad: float32 [4, 2, 3, 64, 16, 32], P('section', None, None, 'seq')
The draws below stay inside these ranges and needn't reach their ends.
All inputs are finite; a program needn't handle non-finite values. No bound on the sum of `events` on one device may be relied on, other than what follows from the above.
Results may differ from the reference program's by a relative error of at most 0.006.
Values may be sent and summed in bfloat16 or wider, within the bound.
No kernel may reach another device: no remote copies, remote signals or barrier semaphores. Data moves between devices by JAX's collectives and lax.ppermute only.
A program may use at most 64 MiB of HBM per device.

```python
import jax
import jax.numpy as jnp
from jax import lax

C = 1024
GROUPS = 64
BINS = 64
GSIZE = 16
NARROW_SPACING = 16
WIDE_SPACING = 256
TOKENS = 1024
N_SECTION = 4


def touch_ends(drawn, own_key, least, largest):
    longest = drawn.shape.index(max(drawn.shape))
    spots = []
    for shift in (0, 1):
        where = [jax.random.randint(jax.random.fold_in(own_key, axis), (), 0, length) for axis, length in enumerate(drawn.shape)]
        where[longest] = (where[longest] + shift) % drawn.shape[longest]
        spots.append(tuple(where))
    return drawn.at[spots[0]].set(least).at[spots[1]].set(largest)


def block_scale(rng, extent, split, low, high):
    def one(dim, shards_of):
        heights = jax.random.uniform(jax.random.fold_in(jax.random.fold_in(rng, 6), dim), (shards_of,), jnp.float32, low / len(split), high / len(split))
        return jnp.repeat(jnp.exp(heights), extent[dim] // shards_of).reshape((-1,) + (1,) * (len(extent) - dim - 1))

    factor_of = one(*split[0])
    for cut in split[1:]:
        factor_of = factor_of * one(*cut)
    return factor_of


def normal_values(stream_key, extent, deviation, bound, shards=(), kind=jnp.bfloat16):
    result = deviation * jax.random.normal(stream_key, extent, jnp.float32)
    if shards:
        result = result * block_scale(stream_key, extent, shards, -0.22, 0.18)
    return jnp.clip(result, -bound, bound).astype(kind)


def setup_inputs(seed: int = 0) -> dict:
    seeds = jax.random.split(jax.random.key(seed), 8)
    return {
        "saved_section_input": normal_values(seeds[0], (N_SECTION, TOKENS, C), 1.0, 6.0, ((0, 4), (1, 8))),
        "out_cot": normal_values(seeds[1], (N_SECTION, TOKENS, C), 1.0, 6.0, ((0, 4), (1, 8))),
        "kernel_weight": normal_values(seeds[2], (N_SECTION, 2, 3, GROUPS, GSIZE, 2 * GSIZE), (3 * GSIZE) ** -0.5, 0.875, ((0, 4),)),
        "blend_weight": normal_values(seeds[3], (N_SECTION, 2, C, C), C ** -0.5, 0.1875, ((0, 4),)),
        "hazard_head": normal_values(seeds[4], (C, BINS), BINS ** -0.5, 0.75),
        "labels": touch_ends(jax.random.randint(seeds[5], (TOKENS,), 0, BINS), jax.random.fold_in(seeds[5], 1), 0, BINS - 1).astype(jnp.int32),
        "events": touch_ends((jax.random.randint(seeds[6], (TOKENS,), 0, 4) < 3).astype(jnp.int32), jax.random.fold_in(seeds[6], 1), 0, 1),
    }


exact_mode = lax.Precision.HIGHEST

def delayed(values, offset):
    zeros = jnp.zeros((offset,) + values.shape[1:], values.dtype)
    return jnp.concatenate([zeros, values[:values.shape[0] - offset]], axis=0)

def advanced(values, offset):
    zeros = jnp.zeros((offset,) + values.shape[1:], values.dtype)
    return jnp.concatenate([values[offset:], zeros], axis=0)

def gate_values(preact):
    filt = preact[..., :GSIZE].astype(jnp.float32)
    gate_part = preact[..., GSIZE:].astype(jnp.float32)
    return jnp.tanh(filt) * jax.nn.sigmoid(gate_part)

def gate_grad(preact, dgated):
    filt = jnp.tanh(preact[..., :GSIZE].astype(jnp.float32))
    gate_part = jax.nn.sigmoid(preact[..., GSIZE:].astype(jnp.float32))
    return jnp.concatenate([dgated * gate_part * (1.0 - filt * filt), dgated * filt * gate_part * (1.0 - gate_part)], axis=-1)

def layer_forward_pass(hidden, weights, mix_matrix, reach):
    total = hidden.shape[0]
    tap_list = [hidden, delayed(hidden, reach), delayed(hidden, 2 * reach)]
    summed = jnp.zeros((total, GROUPS, 2 * GSIZE), jnp.float32)
    for k in range(3):
        summed = summed + jnp.einsum('rgi,gio->rgo', tap_list[k].reshape(total, GROUPS, GSIZE).astype(jnp.float32), weights[k].astype(jnp.float32), precision=exact_mode)
    preact = summed.astype(jnp.bfloat16)
    gated = gate_values(preact).reshape(total, C).astype(jnp.bfloat16)
    output = (hidden.astype(jnp.float32) + jnp.dot(gated, mix_matrix, preferred_element_type=jnp.float32)).astype(jnp.bfloat16)
    return (tap_list, preact, gated, output)

def layer_reverse_pass(upstream_gradient, tap_list, preact, gated, weights, mix_matrix, reach):
    total = upstream_gradient.shape[0]
    dgated = jnp.dot(upstream_gradient, mix_matrix.T, preferred_element_type=jnp.float32).reshape(total, GROUPS, GSIZE)
    dpre = gate_grad(preact, dgated)
    mix_part = jnp.dot(gated.T, upstream_gradient, preferred_element_type=jnp.float32)
    conv_part = jnp.stack([jnp.einsum('rgi,rgo->gio', tap.reshape(total, GROUPS, GSIZE).astype(jnp.float32), dpre, precision=exact_mode) for tap in tap_list])
    back_sum = upstream_gradient.astype(jnp.float32)
    for k in range(3):
        moved = jnp.einsum('rgo,gio->rgi', dpre, weights[k].astype(jnp.float32), precision=exact_mode).reshape(total, C)
        if k > 0:
            moved = advanced(moved, k * reach)
        back_sum = back_sum + moved
    return (back_sum.astype(jnp.bfloat16), mix_part, conv_part)

def reference(saved_section_input, out_cot, kernel_weight, blend_weight, hazard_head, labels, events):
    input_list = []
    mix_list = []
    conv_list = []
    cot_list = []
    for section_number in range(N_SECTION):
        opening_layer = layer_forward_pass(saved_section_input[section_number], kernel_weight[section_number, 0], blend_weight[section_number, 0], NARROW_SPACING)
        closing_layer = layer_forward_pass(opening_layer[3], kernel_weight[section_number, 1], blend_weight[section_number, 1], WIDE_SPACING)
        if section_number == N_SECTION - 1:
            logits = jnp.dot(closing_layer[3], hazard_head, preferred_element_type=jnp.float32)
            hazard = jax.nn.sigmoid(logits)
            bin_ids = jnp.arange(BINS, dtype=jnp.int32)[None, :]
            below = (bin_ids <= labels[:, None]).astype(jnp.float32)
            at_label = (bin_ids == labels[:, None]).astype(jnp.float32) * events[:, None].astype(jnp.float32)
            dlogit = (hazard * below - at_label).astype(jnp.bfloat16)
            loss_cot = jnp.dot(dlogit, hazard_head.T, preferred_element_type=jnp.float32)
            upstream_gradient = (out_cot[section_number].astype(jnp.float32) + loss_cot).astype(jnp.bfloat16)
        else:
            upstream_gradient = out_cot[section_number]
        cot_list.append(upstream_gradient)
        between_gradient, blend_wide, convolution_wide = layer_reverse_pass(upstream_gradient, closing_layer[0], closing_layer[1], closing_layer[2], kernel_weight[section_number, 1], blend_weight[section_number, 1], WIDE_SPACING)
        input_gradient_rows, blend_narrow, convolution_narrow = layer_reverse_pass(between_gradient, opening_layer[0], opening_layer[1], opening_layer[2], kernel_weight[section_number, 0], blend_weight[section_number, 0], NARROW_SPACING)
        input_list.append(input_gradient_rows)
        mix_list.append(jnp.stack([blend_narrow, blend_wide], axis=1))
        conv_list.append(jnp.stack([convolution_narrow, convolution_wide]))
    next_list = input_list[1:] + [cot_list[-1]]
    return (jnp.stack(input_list), jnp.stack(next_list), jnp.stack(mix_list), jnp.stack(conv_list))
```

```python
import functools

import jax
import jax.numpy as jnp
from jax import lax
from jax.experimental import pallas as pl
from jax.experimental.pallas import tpu as pltpu
from jax.sharding import PartitionSpec as P

SPAN = 2
SLAB = 128
F32 = jnp.float32
BF16 = jnp.bfloat16
HALO = 32
REACH = 16


def nn(a, b):
    return lax.dot_general(a, b, (((1,), (0,)), ((), ())), preferred_element_type=F32)


def nt(a, b):
    return lax.dot_general(a, b, (((1,), (1,)), ((), ())), preferred_element_type=F32)


def tn(a, b, precision=None):
    return lax.dot_general(a, b, (((0,), (0,)), ((), ())), preferred_element_type=F32, precision=precision)


def sigmoid(x):
    return 0.5 * jnp.tanh(0.5 * x) + 0.5


def lanes(slab, width=SLAB):
    return pl.ds(pl.multiple_of(slab * width, width), width)


def same_group(group_size):
    rows = lax.broadcasted_iota(jnp.int32, (SLAB, 2 * SLAB), 0) // group_size
    columns = lax.broadcasted_iota(jnp.int32, (SLAB, 2 * SLAB), 1) % SLAB // group_size
    return rows == columns


def spread(group_size, shift, width):
    o = lax.broadcasted_iota(jnp.int32, (width, 2 * SLAB), 0) - shift
    column = lax.broadcasted_iota(jnp.int32, (width, 2 * SLAB), 1)
    return (o == column % group_size + jnp.where(column >= SLAB, group_size, 0)).astype(F32)


def conv(taps, weight):
    acc = nn(jnp.concatenate(taps[:2], axis=1), weight[: 2 * SLAB]) + nn(taps[2], weight[2 * SLAB :])
    return acc.astype(BF16)


def gates(pre):
    pre = pre.astype(F32)
    return jnp.tanh(pre[:, :SLAB]), sigmoid(pre[:, SLAB:])


def gate_grad(tanh, sig, dgated):
    one = dgated * sig
    return jnp.concatenate(
        [(one * (1.0 - tanh * tanh)).astype(BF16), (one * tanh * (1.0 - sig)).astype(BF16)], axis=1
    )


def chunks(blocks, step):
    some = min(blocks, 4)
    if some == blocks:
        step(0, blocks)
    else:
        pl.loop(0, blocks // some)(lambda i: step(i * some, some))


def weight_kernel(group_size, w_ref, out_ref):
    layers, slabs = out_ref.shape[:2]
    one_hot = spread(group_size, 0, 2 * group_size).astype(BF16)
    keep = same_group(group_size)
    for layer in range(layers):
        for k in range(3):
            def one(slab, carry, layer=layer, k=k):
                row = pl.multiple_of((layer * 3 + k) * slabs * SLAB + slab * SLAB, SLAB)
                tiled = nn(w_ref[pl.ds(row, SLAB), :], one_hot)
                out_ref[layer, slab, k * SLAB : (k + 1) * SLAB, :] = jnp.where(keep, tiled, 0.0).astype(BF16)
                return carry
            lax.fori_loop(0, slabs, one, 0)


def forward_kernel(blocks, meta, *refs):
    inputs, tails = refs[:blocks], refs[blocks : 2 * blocks]
    codes, weights, mixes, head, x_ref, mid_ref, pre_ref, gated_ref, dlogit_ref, short_ref = refs[2 * blocks :]
    row_count, channels = inputs[0].shape
    slabs = channels // SLAB
    y = meta[1]
    for p in range(blocks):
        z = meta[3 + p]
        x_ref[z, HALO:, :] = inputs[p][...]
        x_ref[z + 1 - y, :HALO, :] = tails[p][...]

    @pl.when(y == 0)
    def _():
        x_ref[0, :HALO, :] = jnp.zeros((HALO, channels), BF16)

    mid_ref[0:SPAN] = jnp.zeros((SPAN, row_count, channels), BF16)

    def short(first, count):
        rows = count * row_count
        here = pl.ds(first, count)

        def one(slab, carry):
            taps = [
                x_ref[here, HALO - k * REACH : HALO - k * REACH + row_count, lanes(slab)].reshape(rows, SLAB)
                for k in range(3)
            ]
            tanh, sig = gates(conv(taps, weights[0, slab]))
            short_ref[:rows, lanes(slab)] = (tanh * sig).astype(BF16)
            return carry

        lax.fori_loop(0, slabs, one, 0)

        def mix(j, carry):
            column = lanes(j, 256)
            value = x_ref[here, HALO:, column].reshape(rows, 256).astype(F32) + nn(short_ref[:rows, :], mixes[0, :, column])
            mid_ref[pl.ds(first + SPAN, count), :, column] = value.astype(BF16).reshape(count, row_count, 256)
            return carry

        lax.fori_loop(0, channels // 256, mix, 0)

    chunks(blocks, short)

    def long(first, count):
        rows = count * row_count
        here = pl.ds(first, count)

        def one(slab, carry):
            taps = [mid_ref[pl.ds(first + 2 - k, count), :, lanes(slab)].reshape(rows, SLAB) for k in range(3)]
            pre = conv(taps, weights[1, slab])
            pre_ref[here, :, lanes(slab, 2 * SLAB)] = pre.reshape(count, row_count, 2 * SLAB)
            tanh, sig = gates(pre)
            gated_ref[here, :, lanes(slab)] = (tanh * sig).astype(BF16).reshape(count, row_count, SLAB)
            return carry

        lax.fori_loop(0, slabs, one, 0)

    chunks(blocks, long)

    @pl.when(meta[2] == 1)
    def _():
        def hazard(z, carry):
            top = (mid_ref[z + SPAN].astype(F32) + nn(gated_ref[z], mixes[1])).astype(BF16)
            logits = lax.dot_general(head[...], top, (((0,), (1,)), ((), ())), preferred_element_type=F32)
            bins = lax.broadcasted_iota(jnp.int32, logits.shape, 0)
            code = codes[z * SPAN + y]
            label, event = code[0:1, :], code[1:2, :].astype(F32)
            dlogit = jnp.where(bins <= label, jax.nn.sigmoid(logits), 0.0) - jnp.where(bins == label, event, 0.0)
            dlogit_ref[z] = dlogit.astype(BF16)
            return carry

        lax.fori_loop(0, blocks, hazard, 0)

    @pl.when(meta[2] == 0)
    def _():
        dlogit_ref[...] = jnp.zeros(dlogit_ref.shape, BF16)


def weight_sums(group_size, taps, dpre):
    keep = same_group(group_size)
    total = jnp.zeros((SLAB, SLAB), F32)
    for k, tap in enumerate(taps):
        product = jnp.where(keep, tn(tap, dpre), 0.0)
        total = total + lax.dot_general(
            product,
            spread(group_size, 2 * group_size * k, SLAB),
            (((1,), (1,)), ((), ())),
            preferred_element_type=F32,
            precision=lax.Precision.HIGHEST,
        )
    return total


def split_pair(meta, pair, first, total_ref, own_ref, send_ref):
    share = pair // SPAN
    begin = meta[0] * pair - first
    own = pl.multiple_of(begin + meta[1] * share, share)
    other = pl.multiple_of(begin + (1 - meta[1]) * share, share)
    own_ref[...] = total_ref[pl.ds(own, share), :]
    send_ref[...] = total_ref[pl.ds(other, share), :].astype(BF16)


def long_kernel(blocks, group_size, meta, *refs):
    cots = refs[:blocks]
    (mid_ref, pre_ref, gated_ref, dlogit_ref, weights, mixes, head,
     g_ref, between_ref, own_ref, send_ref, d_ref, total_ref) = refs[blocks:]
    row_count, channels = cots[0].shape
    slabs = channels // SLAB
    pair = channels // blocks
    wide = max(pair, SLAB)
    first_slab = meta[0] * pair // SLAB

    @pl.when(meta[2] == 0)
    def _():
        for p in range(blocks):
            g_ref[meta[3 + p]] = cots[p][...]

    @pl.when(meta[2] == 1)
    def _():
        for p in range(blocks):
            z = meta[3 + p]
            loss = lax.dot_general(dlogit_ref[z], head[...], (((0,), (1,)), ((), ())), preferred_element_type=F32)
            g_ref[z] = (cots[p][...].astype(F32) + loss).astype(BF16)

    d_ref[blocks:] = jnp.zeros((SPAN,) + d_ref.shape[1:], BF16)

    def dpre(first, count):
        rows = count * row_count
        here = pl.ds(first, count)

        def one(j, carry):
            dgated = nt(g_ref[here].reshape(rows, channels), mixes[1, lanes(j, 2 * SLAB), :])
            for half in range(2):
                slab = j * 2 + half
                column = lanes(slab, 2 * SLAB)
                tanh, sig = gates(pre_ref[here, :, column].reshape(rows, 2 * SLAB))
                d_ref[here, :, column] = gate_grad(tanh, sig, dgated[:, half * SLAB : (half + 1) * SLAB]).reshape(
                    count, row_count, 2 * SLAB
                )
            return carry

        lax.fori_loop(0, slabs // 2, one, 0)

    chunks(blocks, dpre)

    def back(first, count):
        rows = count * row_count
        here = pl.ds(first, count)

        def one(slab, carry):
            total = g_ref[here, :, lanes(slab)].reshape(rows, SLAB).astype(F32)
            for k in range(3):
                later = d_ref[pl.ds(first + k, count), :, lanes(slab, 2 * SLAB)].reshape(rows, 2 * SLAB)
                total = total + nt(later, weights[1, slab, k * SLAB : (k + 1) * SLAB, :])
            between_ref[here, :, lanes(slab)] = total.astype(BF16).reshape(count, row_count, SLAB)
            return carry

        lax.fori_loop(0, slabs, one, 0)

    chunks(blocks, back)
    all_rows = blocks * row_count
    for i in range(wide // SLAB):
        slab = first_slab + i
        here = slice(i * SLAB, (i + 1) * SLAB)
        total_ref[here, :channels] = tn(
            gated_ref[:, :, lanes(slab)].reshape(all_rows, SLAB), g_ref[...].reshape(all_rows, channels)
        )
        taps = [mid_ref[2 - k : 2 - k + blocks, :, lanes(slab)].reshape(all_rows, SLAB) for k in range(3)]
        total_ref[here, channels:] = weight_sums(
            group_size, taps, d_ref[:blocks, :, lanes(slab, 2 * SLAB)].reshape(all_rows, 2 * SLAB)
        )
    split_pair(meta, pair, first_slab * SLAB, total_ref, own_ref, send_ref)


def own_kernel(meta, x_ref, between_ref, weights, mixes, push_ref, sum_ref, ex_ref):
    row_count, channels = sum_ref.shape
    slabs = channels // SLAB
    z = meta[0]

    def one(j, carry):
        dgated = nt(between_ref[z], mixes[0, lanes(j, 2 * SLAB), :])
        for half in range(2):
            slab = j * 2 + half
            taps = [x_ref[z, HALO - k * REACH : HALO - k * REACH + row_count, lanes(slab)] for k in range(3)]
            tanh, sig = gates(conv(taps, weights[0, slab]))
            dpre = gate_grad(tanh, sig, dgated[:, half * SLAB : (half + 1) * SLAB])
            moved = [nt(dpre, weights[0, slab, k * SLAB : (k + 1) * SLAB, :]) for k in range(3)]
            ex_ref[:HALO, :] = jnp.zeros((HALO, SLAB), F32)
            ex_ref[HALO:, :] = between_ref[z, :, lanes(slab)].astype(F32) + moved[0]
            for k in range(1, 3):
                ex_ref[HALO - k * REACH : HALO - k * REACH + row_count, :] += moved[k]
            push_ref[:, lanes(slab)] = ex_ref[:HALO, :].astype(BF16)
            sum_ref[:, lanes(slab)] = ex_ref[HALO:, :]
        return carry

    lax.fori_loop(0, slabs // 2, one, 0)


def short_kernel(blocks, group_size, meta, x_ref, between_ref, weights, mixes, own_ref, send_ref, total_ref):
    row_count, channels = between_ref.shape[1:]
    pair = channels // blocks
    wide = max(pair, SLAB)
    first_slab = meta[0] * pair // SLAB
    rows = blocks * row_count
    between = between_ref[...].reshape(rows, channels)
    for i in range(wide // SLAB):
        slab = first_slab + i
        here = slice(i * SLAB, (i + 1) * SLAB)
        taps = [
            x_ref[:blocks, HALO - k * REACH : HALO - k * REACH + row_count, lanes(slab)].reshape(rows, SLAB)
            for k in range(3)
        ]
        tanh, sig = gates(conv(taps, weights[0, slab]))
        dpre = gate_grad(tanh, sig, nt(between, mixes[0, lanes(slab), :]))
        total_ref[here, :channels] = tn((tanh * sig).astype(BF16), between)
        total_ref[here, channels:] = weight_sums(group_size, taps, dpre)
    split_pair(meta, pair, first_slab * SLAB, total_ref, own_ref, send_ref)


def finish_kernel(group_size, own0, own1, got0, got1, mix_ref, conv_ref):
    channels = mix_ref.shape[2]
    width = 2 * group_size
    for layer, (own, got) in enumerate(((own0, got0), (own1, got1))):
        total = own[...] + got[...].astype(F32)
        mix_ref[:, layer, :] = total[:, :channels]
        for k in range(3):
            conv_ref[layer, k] = total[:, channels + width * k : channels + width * (k + 1)]


VMEM = pl.BlockSpec(memory_space=pltpu.VMEM)
SMEM = pl.BlockSpec(memory_space=pltpu.SMEM)


def call(kernel, outs, scalars, arrays, scratch=(), name=None, flops=10**8):
    return pl.pallas_call(
        kernel,
        out_shape=[jax.ShapeDtypeStruct(shape, kind) for shape, kind in outs],
        in_specs=[SMEM] * len(scalars) + [VMEM] * len(arrays),
        out_specs=[VMEM] * len(outs),
        scratch_shapes=[pltpu.VMEM(shape, kind) for shape, kind in scratch],
        compiler_params=pltpu.CompilerParams(vmem_limit_bytes=56 * 1024 * 1024),
        cost_estimate=pl.CostEstimate(
            flops=flops, bytes_accessed=sum(a.size * a.dtype.itemsize for a in arrays), transcendentals=0
        ),
        name=name,
    )(*scalars, *arrays)


def body(saved_section_input, out_cot, kernel_weight, blend_weight, hazard_head, labels, events):
    first_input, cot = saved_section_input[0], out_cot[0]
    row_count, channels = first_input.shape
    seq = lax.axis_size("seq")
    blocks = seq // SPAN
    groups, group_size = kernel_weight.shape[3:5]
    slabs = channels // SLAB
    share = channels // seq

    ring = [0] + list(range(1, blocks, 2)) + [b for b in range(blocks - 1, 0, -1) if b % 2 == 0]
    hops = list(zip(ring, ring[1:] + ring[:1]))
    before = {target: source for source, target in hops}
    order = []
    for z in range(blocks):
        arrivals = [z]
        for _ in range(blocks - 1):
            arrivals.append(before[arrivals[-1]])
        order.append(arrivals)

    def step(value):
        return lax.ppermute(
            value, "seq", [(a * SPAN + y, b * SPAN + y) for a, b in hops for y in range(SPAN)]
        )

    def swap(value):
        return lax.ppermute(value, "seq", [(b, b + 1 - 2 * (b % 2)) for b in range(seq)])

    place = lax.axis_index("seq")
    section = lax.axis_index("section")
    is_last = section == lax.axis_size("section") - 1
    z = place // SPAN
    meta = jnp.concatenate(
        [jnp.stack([z, place % SPAN, is_last.astype(jnp.int32)]).astype(jnp.int32), jnp.asarray(order, jnp.int32)[z]]
    )

    inputs, cots = [first_input], [cot]
    tails = [swap(first_input[row_count - HALO :])]
    for _ in range(blocks - 1):
        inputs.append(step(inputs[-1]))
        cots.append(step(cots[-1]))
        tails.append(swap(inputs[-1][row_count - HALO :]))
    codes = lax.all_gather(jnp.stack([labels, events]), "seq")

    (weights,) = call(
        functools.partial(weight_kernel, group_size),
        [((2, slabs, 3 * SLAB, 2 * SLAB), BF16)],
        [],
        [kernel_weight[0].reshape(-1, 2 * group_size)],
        name="weights",
    )
    mixes = blend_weight[0]
    x, mid, pre, gated, dlogit = call(
        functools.partial(forward_kernel, blocks),
        [
            ((blocks + 1, HALO + row_count, channels), BF16),
            ((blocks + SPAN, row_count, channels), BF16),
            ((blocks, row_count, 2 * channels), BF16),
            ((blocks, row_count, channels), BF16),
            ((blocks, hazard_head.shape[1], row_count), BF16),
        ],
        [meta],
        [*inputs, *tails, codes, weights, mixes, hazard_head],
        [((min(blocks, 4) * row_count, channels), BF16)],
        name="forward",
        flops=10**10,
    )
    sums = ((share, channels + SLAB), F32)
    sent = ((share, channels + SLAB), BF16)
    total = ((max(channels // blocks, SLAB), channels + SLAB), F32)
    g, between, own1, send1 = call(
        functools.partial(long_kernel, blocks, group_size),
        [((blocks, row_count, channels), BF16), ((blocks, row_count, channels), BF16), sums, sent],
        [meta],
        [*cots, mid, pre, gated, dlogit, weights, mixes, hazard_head],
        [((blocks + SPAN, row_count, 2 * channels), BF16), total],
        name="long_backward",
        flops=10**10,
    )
    got1 = swap(send1)
    push, own_sum = call(
        own_kernel,
        [((HALO, channels), BF16), ((row_count, channels), F32)],
        [meta],
        [x, between, weights, mixes],
        [((HALO + row_count, SLAB), F32)],
        name="own_backward",
        flops=10**9,
    )
    pushed = lax.ppermute(push, "seq", [(b, b - 1) for b in range(1, seq)])
    own0, send0 = call(
        functools.partial(short_kernel, blocks, group_size),
        [sums, sent],
        [meta],
        [x, between, weights, mixes],
        [total],
        name="short_backward",
        flops=10**9,
    )
    got0 = swap(send0)
    input_gradient = jnp.concatenate(
        [own_sum[: row_count - HALO], own_sum[row_count - HALO :] + pushed.astype(F32)], axis=0
    ).astype(BF16)
    count = lax.axis_size("section")
    received = lax.ppermute(input_gradient, "section", [(s, s - 1) for s in range(1, count)])
    next_cot = jnp.where(is_last, lax.dynamic_index_in_dim(g, z, keepdims=False), received)
    mix_share, conv_share = call(
        functools.partial(finish_kernel, group_size),
        [((share, 2, channels), F32), ((2, 3, share, 2 * group_size), F32)],
        [],
        [own0, own1, got0, got1],
        name="finish",
    )
    conv_share = conv_share.reshape(2, 3, share // group_size, group_size, 2 * group_size)
    return (input_gradient[None], next_cot[None], mix_share[None], conv_share[None])


def solution(mesh):
    return jax.shard_map(
        body,
        mesh=mesh,
        in_specs=(
            P("section", "seq", None),
            P("section", "seq", None),
            P("section", None, None, None, None, None),
            P("section", None, None, None),
            P(),
            P("seq"),
            P("seq"),
        ),
        out_specs=(
            P("section", "seq", None),
            P("section", "seq", None),
            P("section", "seq", None, None),
            P("section", None, None, "seq", None, None),
        ),
        check_vma=False,
    )
```

```python
import functools

import jax
import jax.numpy as jnp
from jax import lax
from jax.experimental import pallas as pl
from jax.experimental.pallas import tpu as pltpu
from jax.sharding import PartitionSpec as P

SPAN = 2
SLAB = 128
F32 = jnp.float32
BF16 = jnp.bfloat16
HALO = 32
REACH = 16


def nn(a, b):
    return lax.dot_general(a, b, (((1,), (0,)), ((), ())), preferred_element_type=F32)


def nt(a, b):
    return lax.dot_general(a, b, (((1,), (1,)), ((), ())), preferred_element_type=F32)


def tn(a, b, precision=None):
    return lax.dot_general(a, b, (((0,), (0,)), ((), ())), preferred_element_type=F32, precision=precision)


def sigmoid(x):
    return 0.5 * jnp.tanh(0.5 * x) + 0.5


def lanes(slab, width=SLAB):
    return pl.ds(pl.multiple_of(slab * width, width), width)


def same_group(group_size):
    rows = lax.broadcasted_iota(jnp.int32, (SLAB, 2 * SLAB), 0) // group_size
    columns = lax.broadcasted_iota(jnp.int32, (SLAB, 2 * SLAB), 1) % SLAB // group_size
    return rows == columns


def spread(group_size, shift, width):
    o = lax.broadcasted_iota(jnp.int32, (width, 2 * SLAB), 0) - shift
    column = lax.broadcasted_iota(jnp.int32, (width, 2 * SLAB), 1)
    return (o == column % group_size + jnp.where(column >= SLAB, group_size, 0)).astype(F32)


def conv(taps, weight):
    return nn(jnp.concatenate(taps, axis=1), weight).astype(BF16)


def gates(pre):
    pre = pre.astype(F32)
    return jnp.tanh(pre[:, :SLAB]), sigmoid(pre[:, SLAB:])


def gate_grad(tanh, sig, dgated):
    one = dgated * sig
    return jnp.concatenate(
        [(one * (1.0 - tanh * tanh)).astype(BF16), (one * tanh * (1.0 - sig)).astype(BF16)], axis=1
    )


def cut(slab, width=SLAB):
    return slice(slab * width, (slab + 1) * width)


def chunks(blocks, step):
    some = min(blocks, 4)
    if some == blocks:
        step(0, blocks)
    else:
        pl.loop(0, blocks // some)(lambda i: step(i * some, some))


def ring_place(index, blocks):
    return jnp.where(index <= blocks // 2, jnp.maximum(2 * index - 1, 0), 2 * (blocks - index))


def arrival(p, blocks):
    z = lax.axis_index("seq") // SPAN
    place = jnp.where(z % 2 == 1, (z + 1) // 2, jnp.where(z == 0, 0, blocks - z // 2))
    return ring_place(lax.rem(place - p + blocks, blocks), blocks)


def on_last_section():
    return lax.axis_index("section") == lax.axis_size("section") - 1


def start_copies(pairs, sems, first=0):
    copies = [pltpu.make_async_copy(source, target, sems.at[first + i]) for i, (source, target) in enumerate(pairs)]
    for copy in copies:
        copy.start()
    return copies


def finish_copies(copies):
    for copy in copies:
        copy.wait()


def weight_kernel(group_size, w_ref, out_ref, fold_ref):
    layers, slabs = out_ref.shape[:2]
    rows = slabs * SLAB
    one_hot = spread(group_size, 0, 2 * group_size).astype(BF16)
    keep = same_group(group_size)
    for layer in range(layers):
        for k in range(3):
            tiled = nn(w_ref[(layer * 3 + k) * rows : (layer * 3 + k + 1) * rows, :], one_hot)
            for slab in range(slabs):
                out_ref[layer, slab, cut(k), :] = jnp.where(keep, tiled[cut(slab)], 0.0).astype(BF16)
    for k in range(3):
        fold_ref[:, cut(k, 2 * SLAB)] = spread(group_size, 2 * group_size * k, SLAB).astype(BF16)


def tail_kernel(value, out_ref):
    out_ref[...] = value[value.shape[0] - HALO :, :]


def forward_kernel(blocks, *refs):
    inputs, tails, codes = refs[:blocks], refs[blocks : 2 * blocks], refs[2 * blocks : 3 * blocks]
    (far_weights, far_mixes, far_head, x_ref, mid_ref, pre_ref, dlogit_ref, weights, mixes, head,
     gated_ref, code_ref, sems) = refs[3 * blocks :]
    row_count, channels = inputs[0].shape
    slabs = channels // SLAB
    y = lax.axis_index("seq") % SPAN
    rows_in = []
    for p in range(blocks):
        z = arrival(p, blocks)
        rows_in.append((inputs[p], x_ref.at[z, pl.ds(HALO, row_count)]))
        rows_in.append((tails[p], x_ref.at[z + 1 - y, pl.ds(0, HALO)]))
    rows_in = start_copies(rows_in, sems)
    held = [(far_weights.at[0], weights.at[0]), (far_mixes.at[0], mixes.at[0]), (far_weights.at[1], weights.at[1])]
    held = start_copies(held + [(far_mixes.at[1], mixes.at[1]), (far_head, head)], sems, 2 * blocks)
    for p in range(blocks):
        code_ref[arrival(p, blocks)] = codes[p][...]
    mid_ref[0:SPAN] = jnp.zeros((SPAN, row_count, channels), BF16)

    @pl.when(y == 0)
    def _():
        x_ref[0, :HALO, :] = jnp.zeros((HALO, channels), BF16)

    finish_copies(rows_in + held[:1])

    def gate(first, count, layer, tap):
        for slab in range(slabs):
            for i in range(count):
                pre = conv([tap(first + i, k, cut(slab)) for k in range(3)], weights[layer, slab])
                if layer:
                    pre_ref[first + i, :, cut(slab, 2 * SLAB)] = pre
                tanh, sig = gates(pre)
                gated_ref[i * row_count : (i + 1) * row_count, cut(slab)] = (tanh * sig).astype(BF16)

    def short_tap(z, k, column):
        return x_ref[z, HALO - k * REACH : HALO - k * REACH + row_count, column]

    def short(first, count):
        gate(first, count, 0, short_tap)
        if count == blocks:
            finish_copies(held[1:2])
        mixed = nn(gated_ref[...], mixes[0]).reshape(count, row_count, channels)
        here = pl.ds(first, count)
        mid_ref[pl.ds(first + SPAN, count)] = (x_ref[here, HALO:, :].astype(F32) + mixed).astype(BF16)

    if blocks > 4:
        finish_copies(held[1:2])
    chunks(blocks, short)
    finish_copies(held[2:])

    def long_tap(z, k, column):
        return mid_ref[z + SPAN - k, :, column]

    def long(first, count):
        gate(first, count, 1, long_tap)

        @pl.when(on_last_section())
        def _():
            for i in range(count):
                z = first + i
                here = slice(i * row_count, (i + 1) * row_count)
                top = (mid_ref[z + SPAN].astype(F32) + nn(gated_ref[here, :], mixes[1])).astype(BF16)
                logits = nt(head[...], top)
                bins = lax.broadcasted_iota(jnp.int32, logits.shape, 0)
                label, event = code_ref[z, 0:1, :], code_ref[z, 1:2, :].astype(F32)
                dlogit = jnp.where(bins <= label, jax.nn.sigmoid(logits), 0.0) - jnp.where(bins == label, event, 0.0)
                dlogit_ref[z] = dlogit.astype(BF16)

    chunks(blocks, long)


def weight_sums(group_size, taps, dpre, fold):
    keep = same_group(group_size)
    product = jnp.concatenate([jnp.where(keep, tn(tap, dpre), 0.0) for tap in taps], axis=1)
    high = product.astype(BF16)
    low = (product - high.astype(F32)).astype(BF16)
    return nt(high, fold) + nt(low, fold)


def pair_slabs(channels, blocks):
    pair = channels // blocks
    return pair, max(pair, SLAB) // SLAB, lax.axis_index("seq") // SPAN * pair // SLAB


def split_pair(pair, total_ref, own_ref, send_ref):
    share = pair // SPAN
    place = lax.axis_index("seq")
    begin = place // SPAN * pair % SLAB if pair < SLAB else 0
    own = pl.multiple_of(begin + place % SPAN * share, share)
    other = pl.multiple_of(begin + (1 - place % SPAN) * share, share)
    own_ref[...] = total_ref[pl.ds(own, share), :]
    send_ref[...] = total_ref[pl.ds(other, share), :].astype(BF16)


def add_loss(z, dlogit_ref, head, g_ref):
    @pl.when(on_last_section())
    def _():
        g_ref[z] = (g_ref[z].astype(F32) + tn(dlogit_ref[z], head[...])).astype(BF16)


def gate_cotangent(z, g_ref, pre_ref, mixes, d_ref):
    for j in range(g_ref.shape[2] // SLAB // 2):
        dgated = nt(g_ref[z], mixes[1, cut(j, 2 * SLAB), :])
        for half in range(2):
            column = cut(j * 2 + half, 2 * SLAB)
            tanh, sig = gates(pre_ref[z, :, column])
            d_ref[z, :, column] = gate_grad(tanh, sig, dgated[:, cut(half)])


def mix_sums(z, g_ref, pre_ref, total_ref):
    channels = g_ref.shape[2]
    _, wide, first_slab = pair_slabs(channels, pre_ref.shape[0])
    for i in range(wide):
        tanh, sig = gates(pre_ref[z, :, lanes(first_slab + i, 2 * SLAB)])
        total_ref[cut(i), :] += tn((tanh * sig).astype(BF16), g_ref[z])


def some(first, end, blocks, step):
    if blocks <= 4:
        for p in range(first, end):
            step(arrival(p, blocks))
    else:
        pl.loop(first, end)(lambda p: step(arrival(p, blocks)))


def early_kernel(blocks, early, *refs):
    cots = refs[:early]
    pre_ref, dlogit_ref, head, mixes, g_ref, d_ref, total_ref, sems = refs[early:]
    copies = start_copies([(cots[p], g_ref.at[arrival(p, blocks)]) for p in range(early)], sems)
    total_ref[...] = jnp.zeros(total_ref.shape, F32)
    finish_copies(copies)

    def one(z):
        add_loss(z, dlogit_ref, head, g_ref)
        gate_cotangent(z, g_ref, pre_ref, mixes, d_ref)
        mix_sums(z, g_ref, pre_ref, total_ref)

    some(0, early, blocks, one)


def mix_kernel(blocks, early, *refs):
    cots, refs = refs[: blocks - early], refs[blocks - early :]
    pre_ref, dlogit_ref, head = refs[:3]
    g_ref, mine_ref, own_ref, send_ref, total_ref, sems = refs[-6:]
    copies = [(cot, g_ref.at[arrival(early + i, blocks)]) for i, cot in enumerate(cots)]
    copies = start_copies(copies, sems)
    total_ref[...] = refs[3][...] if early else jnp.zeros(total_ref.shape, F32)
    finish_copies(copies)

    def one(z):
        add_loss(z, dlogit_ref, head, g_ref)
        mix_sums(z, g_ref, pre_ref, total_ref)

    some(early, blocks, blocks, one)
    mine_ref[...] = g_ref[lax.axis_index("seq") // SPAN]
    split_pair(g_ref.shape[2] // blocks, total_ref, own_ref, send_ref)


def long_kernel(blocks, early, group_size, g_ref, mid_ref, pre_ref, weights, mixes, fold, *refs):
    between_ref, own_ref, send_ref, d_ref, total_ref = refs[-5:]
    row_count, channels = g_ref.shape[1:]
    slabs = channels // SLAB
    pair, wide, first_slab = pair_slabs(channels, blocks)
    d_ref[blocks:] = jnp.zeros((SPAN,) + d_ref.shape[1:], BF16)
    some(early, blocks, blocks, lambda z: gate_cotangent(z, g_ref, pre_ref, mixes, d_ref))

    def back(first, count):
        rows = count * row_count
        here = pl.ds(first, count)
        for slab in range(slabs):
            total = g_ref[here, :, cut(slab)].reshape(rows, SLAB).astype(F32)
            for k in range(3):
                later = d_ref[pl.ds(first + k, count), :, cut(slab, 2 * SLAB)].reshape(rows, 2 * SLAB)
                total = total + nt(later, weights[1, slab, cut(k), :])
            between_ref[here, :, cut(slab)] = total.astype(BF16).reshape(count, row_count, SLAB)

    chunks(blocks, back)
    rows = blocks * row_count
    for i in range(wide):
        slab = first_slab + i
        taps = [mid_ref[2 - k : 2 - k + blocks, :, lanes(slab)].reshape(rows, SLAB) for k in range(3)]
        dpre_part = d_ref[:blocks, :, lanes(slab, 2 * SLAB)].reshape(rows, 2 * SLAB)
        total_ref[cut(i), :] = weight_sums(group_size, taps, dpre_part, fold[...])
    split_pair(pair, total_ref, own_ref, send_ref)


def own_kernel(x_ref, between_ref, weights, mixes, push_ref, sum_ref):
    row_count, channels = sum_ref.shape
    slabs = channels // SLAB
    z = lax.axis_index("seq") // SPAN
    for j in range(slabs // 2):
        dgated = nt(between_ref[z], mixes[0, cut(j, 2 * SLAB), :])
        for half in range(2):
            slab = j * 2 + half
            taps = [x_ref[z, HALO - k * REACH : HALO - k * REACH + row_count, cut(slab)] for k in range(3)]
            tanh, sig = gates(conv(taps, weights[0, slab]))
            dpre = gate_grad(tanh, sig, dgated[:, cut(half)])
            moved = [nt(dpre, weights[0, slab, cut(k), :]) for k in range(3)]
            first = jnp.concatenate([jnp.zeros((REACH, SLAB), F32), moved[1]], axis=0)
            extended = jnp.concatenate([moved[2], jnp.zeros((HALO, SLAB), F32)], axis=0) + jnp.concatenate(
                [first, jnp.zeros((HALO - REACH, SLAB), F32)], axis=0
            )
            push_ref[:, cut(slab)] = extended[:HALO].astype(BF16)
            sum_ref[:, cut(slab)] = between_ref[z, :, cut(slab)].astype(F32) + moved[0] + extended[HALO:]


def short_kernel(blocks, group_size, x_ref, between_ref, weights, mixes, fold, own_ref, send_ref, total_ref):
    row_count, channels = between_ref.shape[1:]
    pair, wide, first_slab = pair_slabs(channels, blocks)
    rows = blocks * row_count
    between = between_ref[...].reshape(rows, channels)
    for i in range(wide):
        slab = first_slab + i
        taps = [
            x_ref[:blocks, HALO - k * REACH : HALO - k * REACH + row_count, lanes(slab)].reshape(rows, SLAB)
            for k in range(3)
        ]
        tanh, sig = gates(conv(taps, weights[0, slab]))
        dpre = gate_grad(tanh, sig, nt(between, mixes[0, lanes(slab), :]))
        total_ref[cut(i), :channels] = tn((tanh * sig).astype(BF16), between)
        total_ref[cut(i), channels:] = weight_sums(group_size, taps, dpre, fold[...])
    split_pair(pair, total_ref, own_ref, send_ref)


def finish_kernel(group_size, mix1, conv1, own0, got_mix1, got_conv1, got0, mix_ref, conv_ref):
    channels = mix_ref.shape[2]
    width = 2 * group_size
    total = own0[...] + got0[...].astype(F32)
    mix_ref[:, 0, :] = total[:, :channels]
    mix_ref[:, 1, :] = mix1[...] + got_mix1[...].astype(F32)
    convs = (total[:, channels:], conv1[...] + got_conv1[...].astype(F32))
    for layer in range(2):
        for k in range(3):
            conv_ref[layer, k] = convs[layer][:, width * k : width * (k + 1)]


VMEM = pl.BlockSpec(memory_space=pltpu.VMEM)
ANY = pl.BlockSpec(memory_space=pl.ANY)


def call(resident, kernel, outs, arrays, scratch=(), name=None, aliases={}, far=(), near=True, us=0.1):
    if resident and near:
        arrays = [a if i in far else pltpu.with_memory_space_constraint(a, pltpu.VMEM) for i, a in enumerate(arrays)]
    make = pltpu.VMEM if resident and near and name != "finish" else jax.ShapeDtypeStruct
    return pl.pallas_call(
        kernel,
        out_shape=[make(shape, kind) for shape, kind in outs],
        in_specs=[ANY if i in far else VMEM for i in range(len(arrays))],
        out_specs=[VMEM] * len(outs),
        scratch_shapes=[pltpu.VMEM(*s) if isinstance(s, tuple) else s for s in scratch],
        input_output_aliases=aliases,
        compiler_params=pltpu.CompilerParams(vmem_limit_bytes=(24 if resident else 56) * 1024 * 1024),
        cost_estimate=pl.CostEstimate(flops=int(us * 1.1e9), bytes_accessed=0, transcendentals=0),
        name=name,
    )(*arrays)


def body(saved_section_input, out_cot, kernel_weight, blend_weight, hazard_head, labels, events):
    first_input, cot = saved_section_input[0], out_cot[0]
    row_count, channels = first_input.shape
    seq = lax.axis_size("seq")
    blocks = seq // SPAN
    groups, group_size = kernel_weight.shape[3:5]
    slabs = channels // SLAB
    share = channels // seq

    ring = [0] + list(range(1, blocks, 2)) + [b for b in range(blocks - 1, 0, -1) if b % 2 == 0]
    hops = list(zip(ring, ring[1:] + ring[:1]))

    def step(value):
        return lax.ppermute(
            value, "seq", [(a * SPAN + y, b * SPAN + y) for a, b in hops for y in range(SPAN)]
        )

    def swap(value):
        return lax.ppermute(value, "seq", [(b, b + 1 - 2 * (b % 2)) for b in range(seq)])

    is_last = on_last_section()

    def direct(value, steps):
        pairs = [(source, source) for source in range(blocks)]
        for _ in range(steps):
            pairs = [(source, dict(hops)[target]) for source, target in pairs]
        return lax.ppermute(value, "seq", [(a * SPAN + y, b * SPAN + y) for a, b in pairs for y in range(SPAN)])

    resident = blocks <= 4
    run = functools.partial(call, resident)
    def tail(value):
        (out,) = run(tail_kernel, [((HALO, channels), BF16)], [value], name="tail", us=0.3)
        return out

    head = hazard_head.T
    tails = [swap(first_input[row_count - HALO :])]
    codes = [jnp.stack([labels, events])]
    weights, fold = run(
        functools.partial(weight_kernel, group_size),
        [((2, slabs, 3 * SLAB, 2 * SLAB), BF16), ((SLAB, 6 * SLAB), BF16)],
        [kernel_weight[0].reshape(-1, 2 * group_size)],
        name="weights",
        near=False,
        us=1.3,
    )
    inputs, cots = [first_input], [cot]
    for p in range(1, blocks):
        inputs.append(step(inputs[-1]))
        tails.append(swap(tail(inputs[-1])))
        codes.append(direct(codes[0], p))
        cots.append(step(cots[-1]))
    mixes = blend_weight[0]
    rows = min(blocks, 4) * row_count
    held = [(a.shape, BF16) for a in (weights, mixes, head)]
    x, mid, pre, dlogit, *kept = run(
        functools.partial(forward_kernel, blocks),
        [
            ((blocks + 1, HALO + row_count, channels), BF16),
            ((blocks + SPAN, row_count, channels), BF16),
            ((blocks, row_count, 2 * channels), BF16),
            ((blocks, head.shape[0], row_count), BF16),
        ]
        + held * resident,
        [*inputs, *tails, *codes, weights, mixes, head],
        held * (not resident)
        + [((rows, channels), BF16), ((blocks, 2, row_count), jnp.int32), pltpu.SemaphoreType.DMA((2 * blocks + 5,))],
        name="forward",
        far=[*range(2 * blocks), *range(3 * blocks, 3 * blocks + 3)],
        us=5,
    )
    if resident:
        weights, mixes, head = kept
    wide = max(channels // blocks, SLAB)
    block_rows = ((blocks, row_count, channels), BF16)
    early = blocks - 1 if resident else 0
    d_rows = ((blocks + SPAN, row_count, 2 * channels), BF16)
    if early:
        g, d, total = run(
            functools.partial(early_kernel, blocks, early),
            [block_rows, d_rows, ((wide, channels), F32)],
            [*cots[:early], pre, dlogit, head, mixes],
            [pltpu.SemaphoreType.DMA((early,))],
            name="early",
            far=range(early),
            us=4,
        )
    late = cots[early:]
    g, mine, mix1, send_mix1 = run(
        functools.partial(mix_kernel, blocks, early),
        [block_rows, ((row_count, channels), BF16), ((share, channels), F32), ((share, channels), BF16)],
        [*late, pre, dlogit, head] + ([total, g] if early else []),
        [((wide, channels), F32), pltpu.SemaphoreType.DMA((len(late),))],
        name="long_mix",
        aliases={len(late) + 4: 0} if early else {},
        far=range(len(late)),
        us=0.7,
    )
    got_mix1 = swap(send_mix1)
    between, conv1, send_conv1, *_ = run(
        functools.partial(long_kernel, blocks, early, group_size),
        [block_rows, ((share, SLAB), F32), ((share, SLAB), BF16)] + ([d_rows] if early else []),
        [g, mid, pre, weights, mixes, fold] + ([d] if early else []),
        ([] if early else [d_rows]) + [((wide, SLAB), F32)],
        name="long_backward",
        aliases={6: 3} if early else {},
        us=3.4,
    )
    got_conv1 = swap(send_conv1)
    push, own_sum = run(
        own_kernel,
        [((HALO, channels), BF16), ((row_count, channels), F32)],
        [x, between, weights, mixes],
        name="own_backward",
        us=2.7,
    )
    pushed = lax.ppermute(push, "seq", [(b, b - 1) for b in range(1, seq)])
    own0, send0 = run(
        functools.partial(short_kernel, blocks, group_size),
        [((share, channels + SLAB), F32), ((share, channels + SLAB), BF16)],
        [x, between, weights, mixes, fold],
        [((wide, channels + SLAB), F32)],
        name="short_backward",
        us=2.5,
    )
    got0 = swap(send0)
    input_gradient = jnp.concatenate(
        [own_sum[: row_count - HALO], own_sum[row_count - HALO :] + pushed.astype(F32)], axis=0
    ).astype(BF16)
    count = lax.axis_size("section")
    received = lax.ppermute(input_gradient, "section", [(s, s - 1) for s in range(1, count)])
    next_cot = jnp.where(is_last, mine, received)
    mix_share, conv_share = run(
        functools.partial(finish_kernel, group_size),
        [((share, 2, channels), F32), ((2, 3, share, 2 * group_size), F32)],
        [mix1, conv1, own0, got_mix1, got_conv1, got0],
        name="finish",
        us=1.4,
    )
    conv_share = conv_share.reshape(2, 3, share // group_size, group_size, 2 * group_size)
    return (input_gradient[None], next_cot[None], mix_share[None], conv_share[None])


def solution(mesh):
    return jax.shard_map(
        body,
        mesh=mesh,
        in_specs=(
            P("section", "seq", None),
            P("section", "seq", None),
            P("section", None, None, None, None, None),
            P("section", None, None, None),
            P(),
            P("seq"),
            P("seq"),
        ),
        out_specs=(
            P("section", "seq", None),
            P("section", "seq", None),
            P("section", "seq", None, None),
            P("section", None, None, "seq", None, None),
        ),
        check_vma=False,
    )
```

```python
import functools

import jax
import jax.numpy as jnp
from jax import lax
from jax.experimental import pallas as pl
from jax.experimental.pallas import tpu as pltpu
from jax.sharding import PartitionSpec as P

SPAN = 2
SLAB = 128
F32 = jnp.float32
BF16 = jnp.bfloat16
HALO = 32
SCALE = 0.5
REACH = 16


def nn(a, b):
    return lax.dot_general(a, b, (((1,), (0,)), ((), ())), preferred_element_type=F32)


def nt(a, b):
    return lax.dot_general(a, b, (((1,), (1,)), ((), ())), preferred_element_type=F32)


def tn(a, b, precision=None):
    return lax.dot_general(a, b, (((0,), (0,)), ((), ())), preferred_element_type=F32, precision=precision)


def sigmoid(x):
    return 0.5 * jnp.tanh(0.5 * x) + 0.5


def lanes(slab, width=SLAB):
    return pl.ds(pl.multiple_of(slab * width, width), width)


def same_group(group_size):
    rows = lax.broadcasted_iota(jnp.int32, (SLAB, 2 * SLAB), 0) // group_size
    columns = lax.broadcasted_iota(jnp.int32, (SLAB, 2 * SLAB), 1) % SLAB // group_size
    return rows == columns


def spread(group_size, shift, width):
    o = lax.broadcasted_iota(jnp.int32, (width, 2 * SLAB), 0) - shift
    column = lax.broadcasted_iota(jnp.int32, (width, 2 * SLAB), 1)
    return (o == column % group_size + jnp.where(column >= SLAB, group_size, 0)).astype(F32)


def conv(taps, weight):
    return nn(jnp.concatenate(taps, axis=1), weight).astype(BF16)


def gates(pre):
    pre = pre.astype(F32)
    return jnp.tanh(pre[:, :SLAB]), sigmoid(pre[:, SLAB:])


def gate_grad(tanh, sig, dgated):
    one = dgated * sig
    return jnp.concatenate(
        [(one * (1.0 - tanh * tanh)).astype(BF16), (one * tanh * (1.0 - sig)).astype(BF16)], axis=1
    )


def cut(slab, width=SLAB):
    return slice(slab * width, (slab + 1) * width)


def chunks(blocks, step):
    some = min(blocks, 4)
    if some == blocks:
        step(0, blocks)
    else:
        pl.loop(0, blocks // some)(lambda i: step(i * some, some))


def ring_place(index, blocks):
    return jnp.where(index <= blocks // 2, jnp.maximum(2 * index - 1, 0), 2 * (blocks - index))


def arrival(p, blocks):
    z = lax.axis_index("seq") // SPAN
    place = jnp.where(z % 2 == 1, (z + 1) // 2, jnp.where(z == 0, 0, blocks - z // 2))
    return ring_place(lax.rem(place - p + blocks, blocks), blocks)


def on_last_section():
    return lax.axis_index("section") == lax.axis_size("section") - 1


def start_copies(pairs, sems, first=0):
    copies = [pltpu.make_async_copy(source, target, sems.at[first + i]) for i, (source, target) in enumerate(pairs)]
    for copy in copies:
        copy.start()
    return copies


def finish_copies(copies):
    for copy in copies:
        copy.wait()


def weight_kernel(group_size, far_w, far_mixes, far_head, far_cot, out_ref, fold_ref, mixes_ref, head_ref, cot_ref,
                  w_ref, sems):
    copies = start_copies([(far_w, w_ref), (far_cot, cot_ref), (far_mixes, mixes_ref), (far_head, head_ref)], sems)
    layers, slabs = out_ref.shape[:2]
    width, groups = w_ref.shape[2:]
    rows = slabs * SLAB
    outputs = 2 * group_size
    row = lax.broadcasted_iota(jnp.int32, (rows, groups), 0)
    pick = (row // group_size == lax.broadcasted_iota(jnp.int32, (rows, groups), 1)).astype(F32).astype(BF16)
    row = lax.broadcasted_iota(jnp.int32, (SLAB, width), 0)
    own = lax.broadcasted_iota(jnp.int32, (SLAB, width), 1) // outputs == row % group_size
    o = lax.broadcasted_iota(jnp.int32, (width, 2 * SLAB), 0) % outputs
    column = lax.broadcasted_iota(jnp.int32, (width, 2 * SLAB), 1)
    one_hot = (o == column % group_size + jnp.where(column >= SLAB, group_size, 0)).astype(F32).astype(BF16)
    keep = same_group(group_size)
    finish_copies(copies[:1])
    for layer in range(layers):
        for k in range(3):
            for slab in range(slabs):
                picked = nt(pick[cut(slab)], w_ref[layer, k])
                tiled = nn(jnp.where(own, picked, 0.0).astype(BF16), one_hot)
                out_ref[layer, slab, cut(k), :] = jnp.where(keep, tiled, 0.0).astype(BF16)
    for k in range(3):
        fold_ref[:, cut(k, 2 * SLAB)] = spread(group_size, outputs * k, SLAB).astype(BF16)
    finish_copies(copies[1:])


def relay_kernel(value, *refs):
    tail_ref, copy_ref, sems = refs[-3:]
    copies = start_copies([(value, copy_ref)], sems)
    tail_ref[...] = value[value.shape[0] - HALO :, :]
    finish_copies(copies)


def forward_kernel(blocks, *refs):
    inputs, tails, codes = refs[:blocks], refs[blocks : 2 * blocks], refs[2 * blocks : 3 * blocks]
    weights, mixes, head, x_ref, mid_ref, pre_ref, dlogit_ref, gated_ref, code_ref, sems = refs[3 * blocks :]
    row_count, channels = inputs[0].shape
    slabs = channels // SLAB
    y = lax.axis_index("seq") % SPAN
    rows_in = []
    for p in range(blocks):
        z = arrival(p, blocks)
        rows_in.append((inputs[p], x_ref.at[z, pl.ds(HALO, row_count)]))
        rows_in.append((tails[p], x_ref.at[z + 1 - y, pl.ds(0, HALO)]))
    rows_in = start_copies(rows_in, sems)
    for p in range(blocks):
        code_ref[arrival(p, blocks)] = codes[p][...]
    mid_ref[0:SPAN] = jnp.zeros((SPAN, row_count, channels), BF16)

    @pl.when(y == 0)
    def _():
        x_ref[0, :HALO, :] = jnp.zeros((HALO, channels), BF16)

    finish_copies(rows_in)

    def gate(first, count, layer, tap):
        for slab in range(slabs):
            for i in range(count):
                pre = conv([tap(first + i, k, cut(slab)) for k in range(3)], weights[layer, slab])
                if layer:
                    pre_ref[first + i, :, cut(slab, 2 * SLAB)] = pre
                tanh, sig = gates(pre)
                gated_ref[i * row_count : (i + 1) * row_count, cut(slab)] = (tanh * sig).astype(BF16)

    def short_tap(z, k, column):
        return x_ref[z, HALO - k * REACH : HALO - k * REACH + row_count, column]

    def short(first, count):
        gate(first, count, 0, short_tap)
        mixed = nn(gated_ref[...], mixes[0]).reshape(count, row_count, channels)
        here = pl.ds(first, count)
        mid_ref[pl.ds(first + SPAN, count)] = (x_ref[here, HALO:, :].astype(F32) + mixed).astype(BF16)

    chunks(blocks, short)

    def long_tap(z, k, column):
        return mid_ref[z + SPAN - k, :, column]

    def long(first, count):
        gate(first, count, 1, long_tap)

        @pl.when(on_last_section())
        def _():
            for i in range(count):
                z = first + i
                here = slice(i * row_count, (i + 1) * row_count)
                top = (mid_ref[z + SPAN].astype(F32) + nn(gated_ref[here, :], mixes[1])).astype(BF16)
                logits = nt(head[...], top)
                bins = lax.broadcasted_iota(jnp.int32, logits.shape, 0)
                label, event = code_ref[z, 0:1, :], code_ref[z, 1:2, :].astype(F32)
                dlogit = jnp.where(bins <= label, jax.nn.sigmoid(logits), 0.0) - jnp.where(bins == label, event, 0.0)
                dlogit_ref[z] = dlogit.astype(BF16)

    chunks(blocks, long)


def weight_sums(group_size, taps, dpre, fold):
    keep = same_group(group_size)
    product = jnp.concatenate([jnp.where(keep, tn(tap, dpre), 0.0) for tap in taps], axis=1)
    high = product.astype(BF16)
    low = (product - high.astype(F32)).astype(BF16)
    return nt(high, fold) + nt(low, fold)


def pair_slabs(channels, blocks):
    pair = channels // blocks
    return pair, max(pair, SLAB) // SLAB, lax.axis_index("seq") // SPAN * pair // SLAB


def split_pair(pair, total_ref, own_ref, send_ref):
    share = pair // SPAN
    place = lax.axis_index("seq")
    begin = place // SPAN * pair % SLAB if pair < SLAB else 0
    own = pl.multiple_of(begin + place % SPAN * share, share)
    other = pl.multiple_of(begin + (1 - place % SPAN) * share, share)
    own_ref[...] = total_ref[pl.ds(own, share), :]
    send_ref[...] = total_ref[pl.ds(other, share), :].astype(BF16)


def add_loss(z, dlogit_ref, head, g_ref):
    @pl.when(on_last_section())
    def _():
        g_ref[z] = (g_ref[z].astype(F32) + tn(dlogit_ref[z], head[...])).astype(BF16)


def gate_cotangent(places, g_ref, pre_ref, mixes, d_ref):
    rows = g_ref.shape[1]
    g = jnp.concatenate([g_ref[z] for z in places], axis=0)
    for j in range(g_ref.shape[2] // SLAB // 2):
        dgated = nt(g, mixes[1, cut(j, 2 * SLAB), :])
        for half in range(2):
            column = cut(j * 2 + half, 2 * SLAB)
            for i, z in enumerate(places):
                tanh, sig = gates(pre_ref[z, :, column])
                d_ref[z, :, column] = gate_grad(tanh, sig, dgated[cut(i, rows), cut(half)])


def mix_sums(places, g_ref, pre_ref, total_ref):
    channels = g_ref.shape[2]
    _, wide, first_slab = pair_slabs(channels, pre_ref.shape[0])
    g = jnp.concatenate([g_ref[z] for z in places], axis=0)
    for i in range(wide):
        gated = []
        for z in places:
            tanh, sig = gates(pre_ref[z, :, lanes(first_slab + i, 2 * SLAB)])
            gated.append((tanh * sig).astype(BF16))
        total_ref[cut(i), :] += tn(jnp.concatenate(gated, axis=0), g)


def some(first, end, blocks, step):
    if blocks <= 4:
        step([arrival(p, blocks) for p in range(first, end)])
    else:
        pl.loop(first, end)(lambda p: step([arrival(p, blocks)]))


def early_kernel(blocks, early, *refs):
    cots = refs[:early]
    pre_ref, dlogit_ref, head, mixes, g_ref, d_ref, total_ref, sems = refs[early:]
    copies = start_copies([(cots[p], g_ref.at[arrival(p, blocks)]) for p in range(early)], sems)
    total_ref[...] = jnp.zeros(total_ref.shape, F32)
    finish_copies(copies)

    def one(places):
        for z in places:
            add_loss(z, dlogit_ref, head, g_ref)
        gate_cotangent(places, g_ref, pre_ref, mixes, d_ref)
        mix_sums(places, g_ref, pre_ref, total_ref)

    some(0, early, blocks, one)


def mix_kernel(blocks, early, *refs):
    cots, refs = refs[: blocks - early], refs[blocks - early :]
    pre_ref, dlogit_ref, head = refs[:3]
    g_ref, mine_ref, own_ref, send_ref, total_ref, sems = refs[-6:]
    copies = [(cot, g_ref.at[arrival(early + i, blocks)]) for i, cot in enumerate(cots)]
    copies = start_copies(copies, sems)
    total_ref[...] = refs[3][...] if early else jnp.zeros(total_ref.shape, F32)
    finish_copies(copies)

    def one(places):
        for z in places:
            add_loss(z, dlogit_ref, head, g_ref)
        mix_sums(places, g_ref, pre_ref, total_ref)

    some(early, blocks, blocks, one)
    mine_ref[...] = g_ref[lax.axis_index("seq") // SPAN]
    split_pair(g_ref.shape[2] // blocks, total_ref, own_ref, send_ref)


def long_conv_sums(blocks, group_size, mid_ref, d_ref, fold, total_ref, columns):
    row_count, channels = mid_ref.shape[1:]
    rows = blocks * row_count
    _, wide, first_slab = pair_slabs(channels, blocks)
    for i in range(wide):
        slab = first_slab + i
        taps = [mid_ref[2 - k : 2 - k + blocks, :, lanes(slab)].reshape(rows, SLAB) for k in range(3)]
        dpre_part = d_ref[:blocks, :, lanes(slab, 2 * SLAB)].reshape(rows, 2 * SLAB)
        total_ref[cut(i), columns] = weight_sums(group_size, taps, dpre_part, fold[...])


def long_kernel(blocks, early, group_size, g_ref, mid_ref, pre_ref, weights, mixes, fold, *refs):
    between_ref, last_ref = refs[-3:-1] if early else refs[:2]
    d_ref = last_ref if early else refs[2]
    row_count, channels = g_ref.shape[1:]
    slabs = channels // SLAB
    d_ref[blocks:] = jnp.zeros((SPAN,) + d_ref.shape[1:], BF16)
    some(early, blocks, blocks, lambda places: gate_cotangent(places, g_ref, pre_ref, mixes, d_ref))

    def back(first, count):
        rows = count * row_count
        here = pl.ds(first, count)
        for slab in range(slabs):
            total = g_ref[here, :, cut(slab)].reshape(rows, SLAB).astype(F32)
            for k in range(3):
                later = d_ref[pl.ds(first + k, count), :, cut(slab, 2 * SLAB)].reshape(rows, 2 * SLAB)
                total = total + nt(later, weights[1, slab, cut(k), :])
            between_ref[here, :, cut(slab)] = total.astype(BF16).reshape(count, row_count, SLAB)

    chunks(blocks, back)
    if not early:
        long_conv_sums(blocks, group_size, mid_ref, d_ref, fold, last_ref, slice(0, SLAB))


def own_kernel(x_ref, between_ref, weights, mixes, push_ref, sum_ref):
    row_count, channels = sum_ref.shape
    slabs = channels // SLAB
    z = lax.axis_index("seq") // SPAN
    for j in range(slabs // 2):
        dgated = nt(between_ref[z], mixes[0, cut(j, 2 * SLAB), :])
        for half in range(2):
            slab = j * 2 + half
            taps = [x_ref[z, HALO - k * REACH : HALO - k * REACH + row_count, cut(slab)] for k in range(3)]
            tanh, sig = gates(conv(taps, weights[0, slab]))
            dpre = gate_grad(tanh, sig, dgated[:, cut(half)])
            moved = [nt(dpre, weights[0, slab, cut(k), :]) for k in range(3)]
            first = jnp.concatenate([jnp.zeros((REACH, SLAB), F32), moved[1]], axis=0)
            extended = jnp.concatenate([moved[2], jnp.zeros((HALO, SLAB), F32)], axis=0) + jnp.concatenate(
                [first, jnp.zeros((HALO - REACH, SLAB), F32)], axis=0
            )
            push_ref[:, cut(slab)] = extended[:HALO].astype(BF16)
            sum_ref[:, cut(slab)] = between_ref[z, :, cut(slab)].astype(F32) + moved[0] + extended[HALO:]


def short_kernel(blocks, group_size, x_ref, between_ref, weights, mixes, fold, *refs):
    *long_refs, _, _, own_ref, send_ref, total_ref = refs
    row_count, channels = between_ref.shape[1:]
    pair, wide, first_slab = pair_slabs(channels, blocks)
    rows = blocks * row_count
    between = between_ref[...].reshape(rows, channels)
    for i in range(wide):
        slab = first_slab + i
        taps = [
            x_ref[:blocks, HALO - k * REACH : HALO - k * REACH + row_count, lanes(slab)].reshape(rows, SLAB)
            for k in range(3)
        ]
        tanh, sig = gates(conv(taps, weights[0, slab]))
        dpre = gate_grad(tanh, sig, nt(between, mixes[0, lanes(slab), :]))
        total_ref[cut(i), :channels] = tn((tanh * sig).astype(BF16), between)
        total_ref[cut(i), channels : channels + SLAB] = weight_sums(group_size, taps, dpre, fold[...])
    last = slice(channels + SLAB, channels + 2 * SLAB)
    if len(long_refs) > 1:
        long_conv_sums(blocks, group_size, *long_refs, fold, total_ref, last)
    else:
        total_ref[:, last] = long_refs[0][...]
    split_pair(pair, total_ref, own_ref, send_ref)


def finish_kernel(group_size, mix1, own0, got_mix1, got0, mix_ref, conv_ref):
    channels = mix_ref.shape[2]
    width = 2 * group_size
    total = own0[...] + got0[...].astype(F32)
    mix_ref[:, 0, :] = total[:, :channels]
    mix_ref[:, 1, :] = mix1[...] + got_mix1[...].astype(F32)
    for layer in range(2):
        for k in range(3):
            begin = channels + SLAB * layer + width * k
            conv_ref[layer, k] = total[:, begin : begin + width]


def add_kernel(own_ref, pushed_ref, out_ref):
    rest = out_ref.shape[0] - HALO
    out_ref[:rest, :] = own_ref[:rest, :].astype(BF16)
    out_ref[rest:, :] = (own_ref[rest:, :] + pushed_ref[...].astype(F32)).astype(BF16)


def choose_kernel(last_ref, other_ref, out_ref):
    out_ref[...] = jnp.where(on_last_section(), last_ref[...].astype(F32), other_ref[...].astype(F32)).astype(BF16)


VMEM = pl.BlockSpec(memory_space=pltpu.VMEM)
ANY = pl.BlockSpec(memory_space=pl.ANY)


def call(resident, kernel, outs, arrays, scratch=(), name=None, aliases={}, far=(), near=True, final=False, us=0.1):
    if resident and near:
        arrays = [a if i in far else pltpu.with_memory_space_constraint(a, pltpu.VMEM) for i, a in enumerate(arrays)]
    make = pltpu.VMEM if resident and near and not final else jax.ShapeDtypeStruct
    return pl.pallas_call(
        kernel,
        out_shape=[make(shape, kind) for shape, kind in outs],
        in_specs=[ANY if i in far else VMEM for i in range(len(arrays))],
        out_specs=[VMEM] * len(outs),
        scratch_shapes=[pltpu.VMEM(*s) if isinstance(s, tuple) else s for s in scratch],
        input_output_aliases=aliases,
        compiler_params=pltpu.CompilerParams(vmem_limit_bytes=(24 if resident else 56) * 1024 * 1024),
        cost_estimate=pl.CostEstimate(flops=int(us * SCALE * 1.1e9), bytes_accessed=0, transcendentals=0),
        name=name,
    )(*arrays)


def body(saved_section_input, out_cot, kernel_weight, blend_weight, hazard_head, labels, events):
    first_input, cot = saved_section_input[0], out_cot[0]
    row_count, channels = first_input.shape
    seq = lax.axis_size("seq")
    blocks = seq // SPAN
    groups, group_size = kernel_weight.shape[3:5]
    slabs = channels // SLAB
    share = channels // seq

    ring = [0] + list(range(1, blocks, 2)) + [b for b in range(blocks - 1, 0, -1) if b % 2 == 0]
    hops = list(zip(ring, ring[1:] + ring[:1]))

    def step(value):
        return lax.ppermute(
            value, "seq", [(a * SPAN + y, b * SPAN + y) for a, b in hops for y in range(SPAN)]
        )

    def swap(value):
        return lax.ppermute(value, "seq", [(b, b + 1 - 2 * (b % 2)) for b in range(seq)])

    def direct(value, steps):
        pairs = [(source, source) for source in range(blocks)]
        for _ in range(steps):
            pairs = [(source, dict(hops)[target]) for source, target in pairs]
        return lax.ppermute(value, "seq", [(a * SPAN + y, b * SPAN + y) for a, b in pairs for y in range(SPAN)])

    resident = blocks <= 4
    run = functools.partial(call, resident)
    def relay(value, *others):
        return run(
            relay_kernel,
            [((HALO, channels), BF16), ((row_count, channels), BF16)],
            [value, *others],
            [pltpu.SemaphoreType.DMA((1,))],
            name="relay",
            far=range(1, 1 + len(others)),
            us=0.3,
        )

    def far(value):
        return pltpu.with_memory_space_constraint(value, pltpu.HBM) if resident else value

    head = far(hazard_head.T)
    tails = [swap(first_input[row_count - HALO :])]
    codes = [jnp.stack([labels, events])]
    taps = far(kernel_weight[0].transpose(0, 1, 3, 4, 2).reshape(2, 3, -1, groups))
    mixes, far_cot = far(blend_weight[0]), far(cot)
    weights, fold, mixes, head, own_cot = run(
        functools.partial(weight_kernel, group_size),
        [((2, slabs, 3 * SLAB, 2 * SLAB), BF16), ((SLAB, 6 * SLAB), BF16), (mixes.shape, BF16), (head.shape, BF16), (cot.shape, BF16)],
        [taps, mixes, head, far_cot],
        [(taps.shape, BF16), pltpu.SemaphoreType.DMA((4,))],
        name="weights",
        far=(0, 1, 2, 3),
        us=3.5,
    )
    inputs, cots = [first_input], [cot]
    codes += [direct(codes[0], p) for p in range(1, blocks)]
    before = {1: [tails[0], fold], 2: codes[1:]}
    sent_input = first_input
    cots.append(step(own_cot))
    for p in range(1, blocks):
        inputs.append(step(sent_input))
        if p > 1:
            cots.append(step(cots[-1]))
        tail, sent_input = relay(inputs[-1], *before.get(p, []))
        tails.append(swap(tail))
    rows = min(blocks, 4) * row_count
    x, mid, pre, dlogit = run(
        functools.partial(forward_kernel, blocks),
        [
            ((blocks + 1, HALO + row_count, channels), BF16),
            ((blocks + SPAN, row_count, channels), BF16),
            ((blocks, row_count, 2 * channels), BF16),
            ((blocks, head.shape[0], row_count), BF16),
        ],
        [far(first_input), *inputs[1:], *tails, *codes, weights, mixes, head],
        [((rows, channels), BF16), ((blocks, 2, row_count), jnp.int32), pltpu.SemaphoreType.DMA((2 * blocks,))],
        name="forward",
        far=range(2 * blocks),
        us=5,
    )
    wide = max(channels // blocks, SLAB)
    block_rows = ((blocks, row_count, channels), BF16)
    early = blocks - 1 if resident else 0
    d_rows = ((blocks + SPAN, row_count, 2 * channels), BF16)
    if early:
        g, d, total = run(
            functools.partial(early_kernel, blocks, early),
            [block_rows, d_rows, ((wide, channels), F32)],
            [far_cot, *cots[1:early], pre, dlogit, head, mixes],
            [pltpu.SemaphoreType.DMA((early,))],
            name="early",
            far=range(early),
            us=4,
        )
    late = cots[early:]
    g, mine, mix1, send_mix1 = run(
        functools.partial(mix_kernel, blocks, early),
        [block_rows, ((row_count, channels), BF16), ((share, channels), F32), ((share, channels), BF16)],
        [*late, pre, dlogit, head] + ([total, g] if early else []),
        [((wide, channels), F32), pltpu.SemaphoreType.DMA((len(late),))],
        name="long_mix",
        aliases={len(late) + 4: 0} if early else {},
        far=range(len(late)),
        us=0.7,
    )
    got_mix1 = swap(send_mix1)
    between, last = run(
        functools.partial(long_kernel, blocks, early, group_size),
        [block_rows, d_rows if early else ((wide, SLAB), F32)],
        [g, mid, pre, weights, mixes, fold] + ([d] if early else []),
        [((8, SLAB), F32) if early else d_rows],
        name="long_backward",
        aliases={6: 1} if early else {},
        us=3.4,
    )
    push, own_sum = run(
        own_kernel,
        [((HALO, channels), BF16), ((row_count, channels), F32)],
        [x, between, weights, mixes],
        name="own_backward",
        us=2.7,
    )
    pushed = lax.ppermute(push, "seq", [(b, b - 1) for b in range(1, seq)])
    sums = channels + 2 * SLAB
    own0, send0 = run(
        functools.partial(short_kernel, blocks, group_size),
        [((share, sums), F32), ((share, sums), BF16)],
        [x, between, weights, mixes, fold] + ([mid, last] if early else [last]) + [push, got_mix1],
        [((wide, sums), F32)],
        name="short_backward",
        far=(7, 8) if early else (6, 7),
        us=2.5,
    )
    got0 = swap(send0)
    rows_out = ((row_count, channels), BF16)
    (input_gradient,) = run(add_kernel, [rows_out], [own_sum, pushed], name="add", final=True, us=0.4)
    count = lax.axis_size("section")
    received = lax.ppermute(input_gradient, "section", [(s, s - 1) for s in range(1, count)])
    (next_cot,) = run(choose_kernel, [rows_out], [mine, received], name="choose", final=True, us=0.4)
    mix_share, conv_share = run(
        functools.partial(finish_kernel, group_size),
        [((share, 2, channels), F32), ((2, 3, share, 2 * group_size), F32)],
        [mix1, own0, got_mix1, got0],
        name="finish",
        final=True,
        us=1.4,
    )
    conv_share = conv_share.reshape(2, 3, share // group_size, group_size, 2 * group_size)
    return (input_gradient[None], next_cot[None], mix_share[None], conv_share[None])


def solution(mesh):
    return jax.shard_map(
        body,
        mesh=mesh,
        in_specs=(
            P("section", "seq", None),
            P("section", "seq", None),
            P("section", None, None, None, None, None),
            P("section", None, None, None),
            P(),
            P("seq"),
            P("seq"),
        ),
        out_specs=(
            P("section", "seq", None),
            P("section", "seq", None),
            P("section", "seq", None, None),
            P("section", None, None, "seq", None, None),
        ),
        check_vma=False,
    )
```

```python
import functools

import jax
import jax.numpy as jnp
from jax import lax
from jax.experimental import pallas as pl
from jax.experimental.pallas import tpu as pltpu
from jax.sharding import PartitionSpec as P

SPAN = 2
SLAB = 128
F32 = jnp.float32
BF16 = jnp.bfloat16
HALO = 32
CODE_ROWS = 16
SCALE = 0.5
REACH = 16


def nn(a, b):
    return lax.dot_general(a, b, (((1,), (0,)), ((), ())), preferred_element_type=F32)


def nt(a, b):
    return lax.dot_general(a, b, (((1,), (1,)), ((), ())), preferred_element_type=F32)


def tn(a, b, precision=None):
    return lax.dot_general(a, b, (((0,), (0,)), ((), ())), preferred_element_type=F32, precision=precision)


def sigmoid(x):
    return 0.5 * jnp.tanh(0.5 * x) + 0.5


def lanes(slab, width=SLAB):
    return pl.ds(pl.multiple_of(slab * width, width), width)


def same_group(group_size):
    rows = lax.broadcasted_iota(jnp.int32, (SLAB, 2 * SLAB), 0) // group_size
    columns = lax.broadcasted_iota(jnp.int32, (SLAB, 2 * SLAB), 1) % SLAB // group_size
    return rows == columns


def spread(group_size, shift, width):
    o = lax.broadcasted_iota(jnp.int32, (width, 2 * SLAB), 0) - shift
    column = lax.broadcasted_iota(jnp.int32, (width, 2 * SLAB), 1)
    return (o == column % group_size + jnp.where(column >= SLAB, group_size, 0)).astype(F32)


def conv(taps, weight):
    return nn(jnp.concatenate(taps, axis=1), weight).astype(BF16)


def gates(pre):
    pre = pre.astype(F32)
    return jnp.tanh(pre[:, :SLAB]), sigmoid(pre[:, SLAB:])


def gate_grad(tanh, sig, dgated):
    one = dgated * sig
    return jnp.concatenate(
        [(one * (1.0 - tanh * tanh)).astype(BF16), (one * tanh * (1.0 - sig)).astype(BF16)], axis=1
    )


def cut(slab, width=SLAB):
    return slice(slab * width, (slab + 1) * width)


def chunks(blocks, step):
    some = min(blocks, 4)
    if some == blocks:
        step(0, blocks)
    else:
        pl.loop(0, blocks // some)(lambda i: step(i * some, some))


def ring_place(index, blocks):
    return jnp.where(index <= blocks // 2, jnp.maximum(2 * index - 1, 0), 2 * (blocks - index))


def arrival(p, blocks):
    z = lax.axis_index("seq") // SPAN
    place = jnp.where(z % 2 == 1, (z + 1) // 2, jnp.where(z == 0, 0, blocks - z // 2))
    return ring_place(lax.rem(place - p + blocks, blocks), blocks)


def on_last_section():
    return lax.axis_index("section") == lax.axis_size("section") - 1


def start_copies(pairs, sems, first=0):
    copies = [pltpu.make_async_copy(source, target, sems.at[first + i]) for i, (source, target) in enumerate(pairs)]
    for copy in copies:
        copy.start()
    return copies


def finish_copies(copies):
    for copy in copies:
        copy.wait()


def weight_kernel(group_size, far_w, far_mixes, far_head, far_cot, far_labels, far_events, out_ref, fold_ref, mixes_ref,
                  head_ref, cot_ref, w_ref, labels, events, sems):
    row_count = far_cot.shape[0]
    copies = [(far_w, w_ref), (far_labels, labels), (far_events, events), (far_cot, cot_ref.at[pl.ds(0, row_count)])]
    copies = start_copies(copies + [(far_mixes, mixes_ref), (far_head, head_ref)], sems)
    layers, slabs = out_ref.shape[:2]
    width, groups = w_ref.shape[2:]
    rows = slabs * SLAB
    outputs = 2 * group_size
    row = lax.broadcasted_iota(jnp.int32, (rows, groups), 0)
    pick = (row // group_size == lax.broadcasted_iota(jnp.int32, (rows, groups), 1)).astype(F32).astype(BF16)
    row = lax.broadcasted_iota(jnp.int32, (SLAB, width), 0)
    own = lax.broadcasted_iota(jnp.int32, (SLAB, width), 1) // outputs == row % group_size
    o = lax.broadcasted_iota(jnp.int32, (width, 2 * SLAB), 0) % outputs
    column = lax.broadcasted_iota(jnp.int32, (width, 2 * SLAB), 1)
    one_hot = (o == column % group_size + jnp.where(column >= SLAB, group_size, 0)).astype(F32).astype(BF16)
    keep = same_group(group_size)
    cot_ref[row_count:, :] = jnp.zeros((CODE_ROWS, cot_ref.shape[1]), BF16)
    finish_copies(copies[:3])
    code = (labels[...] + head_ref.shape[0] * events[...]).astype(F32)
    cot_ref[row_count:, :row_count] = jnp.broadcast_to(code, (CODE_ROWS, row_count)).astype(BF16)
    for layer in range(layers):
        for k in range(3):
            for slab in range(slabs):
                picked = nt(pick[cut(slab)], w_ref[layer, k])
                tiled = nn(jnp.where(own, picked, 0.0).astype(BF16), one_hot)
                out_ref[layer, slab, cut(k), :] = jnp.where(keep, tiled, 0.0).astype(BF16)
    for k in range(3):
        fold_ref[:, cut(k, 2 * SLAB)] = spread(group_size, outputs * k, SLAB).astype(BF16)
    finish_copies(copies[3:])


def relay_kernel(copied, *refs):
    *copy_refs, tail_ref, sems = refs[-(2 + copied) :]
    copies = start_copies(list(zip(refs[:copied], copy_refs)), sems)
    tail_ref[...] = refs[0][refs[0].shape[0] - HALO :, :]
    finish_copies(copies)


def short_rows(places, begin, end, x_ref, mid_ref, weights, mixes, gated_ref):
    channels, length = x_ref.shape[2], end - begin
    for slab in range(channels // SLAB):
        for i, z in enumerate(places):
            at = [HALO + begin - k * REACH for k in range(3)]
            tanh, sig = gates(conv([x_ref[z, j : j + length, cut(slab)] for j in at], weights[0, slab]))
            gated_ref[cut(i, length), cut(slab)] = (tanh * sig).astype(BF16)
    mixed = nn(gated_ref[: len(places) * length, :], mixes[0])
    for i, z in enumerate(places):
        here = x_ref[z, HALO + begin : HALO + end, :]
        mid_ref[z + SPAN, begin:end, :] = (here.astype(F32) + mixed[cut(i, length)]).astype(BF16)


def begin_kernel(blocks, first, count, inputs, weights, mixes, x_ref, mid_ref, gated_ref, sems):
    row_count = inputs[0].shape[0]
    places = [arrival(first + i, blocks) for i in range(count)]
    copies = start_copies([(a, x_ref.at[z, pl.ds(HALO, row_count)]) for a, z in zip(inputs, places)], sems)
    if first == 0:
        mid_ref[0:SPAN] = jnp.zeros((SPAN,) + mid_ref.shape[1:], BF16)
    finish_copies(copies)
    if count <= 4:
        short_rows(places, HALO, row_count, x_ref, mid_ref, weights, mixes, gated_ref)
    else:
        some(first, first + count, blocks,
             lambda places: short_rows(places, HALO, row_count, x_ref, mid_ref, weights, mixes, gated_ref))


def begin_some(blocks, first, count, *refs):
    x_ref, mid_ref, gated_ref, sems = refs[-4:]
    begin_kernel(blocks, first, count, refs[:count], refs[count], refs[count + 1], x_ref, mid_ref, gated_ref, sems)


def forward_kernel(blocks, resident, *refs):
    inputs, refs = ([], refs) if resident else (refs[:blocks], refs[blocks:])
    tails, refs = refs[:blocks], refs[blocks:]
    weights, mixes, head = refs[:3]
    x_ref, mid_ref, pre_ref, hazard_ref, gated_ref, sems = refs[-6:]
    row_count, channels = mid_ref.shape[1:]
    y = lax.axis_index("seq") % SPAN
    copies = [(tails[p], x_ref.at[arrival(p, blocks) + 1 - y, pl.ds(0, HALO)]) for p in range(blocks)]
    copies = start_copies(copies, sems)
    if not resident:
        late = sems.at[pl.ds(blocks, blocks)]
        begin_kernel(blocks, 0, blocks, inputs, weights, mixes, x_ref, mid_ref, gated_ref, late)

    @pl.when(y == 0)
    def _():
        x_ref[0, :HALO, :] = jnp.zeros((HALO, channels), BF16)

    finish_copies(copies)

    def short(first, count):
        places = [first + i for i in range(count)]
        short_rows(places, 0, HALO, x_ref, mid_ref, weights, mixes, gated_ref)

    chunks(blocks, short)

    def long(first, count):
        for slab in range(channels // SLAB):
            for i in range(count):
                pre = conv([mid_ref[first + i + SPAN - k, :, cut(slab)] for k in range(3)], weights[1, slab])
                pre_ref[first + i, :, cut(slab, 2 * SLAB)] = pre
                tanh, sig = gates(pre)
                gated_ref[cut(i, row_count), cut(slab)] = (tanh * sig).astype(BF16)

        @pl.when(on_last_section())
        def _():
            mixed = nn(gated_ref[...], mixes[1])
            for i in range(count):
                top = (mid_ref[first + i + SPAN].astype(F32) + mixed[cut(i, row_count)]).astype(BF16)
                hazard_ref[first + i] = jax.nn.sigmoid(nt(head[...], top))

    chunks(blocks, long)


def weight_sums(group_size, taps, dpre, fold):
    keep = same_group(group_size)
    product = jnp.concatenate([jnp.where(keep, tn(tap, dpre), 0.0) for tap in taps], axis=1)
    high = product.astype(BF16)
    low = (product - high.astype(F32)).astype(BF16)
    return nt(high, fold) + nt(low, fold)


def pair_slabs(channels, blocks):
    pair = channels // blocks
    return pair, max(pair, SLAB) // SLAB, lax.axis_index("seq") // SPAN * pair // SLAB


def split_pair(pair, total_ref, own_ref, send_ref):
    share = pair // SPAN
    place = lax.axis_index("seq")
    begin = place // SPAN * pair % SLAB if pair < SLAB else 0
    own = pl.multiple_of(begin + place % SPAN * share, share)
    other = pl.multiple_of(begin + (1 - place % SPAN) * share, share)
    own_ref[...] = total_ref[pl.ds(own, share), :]
    send_ref[...] = total_ref[pl.ds(other, share), :].astype(BF16)


def fetch_cotangents(cots, first, blocks, g_ref, code_ref, sems):
    row_count = g_ref.shape[1]
    copies = []
    for i, cot in enumerate(cots):
        z = arrival(first + i, blocks)
        copies.append((cot.at[pl.ds(0, row_count)], g_ref.at[z]))
        copies.append((cot.at[pl.ds(row_count, CODE_ROWS), pl.ds(0, row_count)], code_ref.at[z]))
    return start_copies(copies, sems)


def add_loss(places, code_ref, hazard_ref, head, g_ref):
    @pl.when(on_last_section())
    def _():
        for z in places:
            hazard = hazard_ref[z]
            bins = lax.broadcasted_iota(jnp.int32, hazard.shape, 0).astype(F32)
            code = code_ref[z, 0:1, :].astype(F32)
            event = jnp.where(code >= hazard.shape[0], 1.0, 0.0)
            label = code - hazard.shape[0] * event
            dlogit = jnp.where(bins <= label, hazard, 0.0) - jnp.where(bins == label, event, 0.0)
            g_ref[z] = (g_ref[z].astype(F32) + tn(dlogit.astype(BF16), head[...])).astype(BF16)


def gate_cotangent(places, g_ref, pre_ref, mixes, d_ref):
    rows = g_ref.shape[1]
    g = jnp.concatenate([g_ref[z] for z in places], axis=0)
    for j in range(g_ref.shape[2] // SLAB // 2):
        dgated = nt(g, mixes[1, cut(j, 2 * SLAB), :])
        for half in range(2):
            column = cut(j * 2 + half, 2 * SLAB)
            for i, z in enumerate(places):
                tanh, sig = gates(pre_ref[z, :, column])
                d_ref[z, :, column] = gate_grad(tanh, sig, dgated[cut(i, rows), cut(half)])


def mix_sums(places, g_ref, pre_ref, total_ref):
    channels = g_ref.shape[2]
    _, wide, first_slab = pair_slabs(channels, pre_ref.shape[0])
    g = jnp.concatenate([g_ref[z] for z in places], axis=0)
    for i in range(wide):
        gated = []
        for z in places:
            tanh, sig = gates(pre_ref[z, :, lanes(first_slab + i, 2 * SLAB)])
            gated.append((tanh * sig).astype(BF16))
        total_ref[cut(i), :] += tn(jnp.concatenate(gated, axis=0), g)


def some(first, end, blocks, step):
    if blocks <= 4:
        step([arrival(p, blocks) for p in range(first, end)])
    else:
        pl.loop(first, end)(lambda p: step([arrival(p, blocks)]))


def early_kernel(blocks, early, *refs):
    cots = refs[:early]
    pre_ref, hazard_ref, head, mixes, g_ref, d_ref, total_ref, code_ref, sems = refs[early:]
    copies = fetch_cotangents(cots, 0, blocks, g_ref, code_ref, sems)
    total_ref[...] = jnp.zeros(total_ref.shape, F32)
    finish_copies(copies)

    def one(places):
        add_loss(places, code_ref, hazard_ref, head, g_ref)
        gate_cotangent(places, g_ref, pre_ref, mixes, d_ref)
        mix_sums(places, g_ref, pre_ref, total_ref)

    some(0, early, blocks, one)


def mix_kernel(blocks, early, *refs):
    cots, refs = refs[: blocks - early], refs[blocks - early :]
    pre_ref, hazard_ref, head = refs[:3]
    g_ref, mine_ref, own_ref, send_ref, total_ref, code_ref, sems = refs[-7:]
    copies = fetch_cotangents(cots, early, blocks, g_ref, code_ref, sems)
    total_ref[...] = refs[3][...] if early else jnp.zeros(total_ref.shape, F32)
    finish_copies(copies)

    def one(places):
        add_loss(places, code_ref, hazard_ref, head, g_ref)
        mix_sums(places, g_ref, pre_ref, total_ref)

    some(early, blocks, blocks, one)
    mine_ref[...] = g_ref[lax.axis_index("seq") // SPAN]
    split_pair(g_ref.shape[2] // blocks, total_ref, own_ref, send_ref)


def long_conv_sums(blocks, group_size, mid_ref, d_ref, fold, total_ref, columns):
    row_count, channels = mid_ref.shape[1:]
    rows = blocks * row_count
    _, wide, first_slab = pair_slabs(channels, blocks)
    for i in range(wide):
        slab = first_slab + i
        taps = [mid_ref[2 - k : 2 - k + blocks, :, lanes(slab)].reshape(rows, SLAB) for k in range(3)]
        dpre_part = d_ref[:blocks, :, lanes(slab, 2 * SLAB)].reshape(rows, 2 * SLAB)
        total_ref[cut(i), columns] = weight_sums(group_size, taps, dpre_part, fold[...])


def long_kernel(blocks, early, group_size, g_ref, mid_ref, pre_ref, weights, mixes, fold, *refs):
    between_ref, last_ref = refs[-3:-1] if early else refs[:2]
    d_ref = last_ref if early else refs[2]
    row_count, channels = g_ref.shape[1:]
    slabs = channels // SLAB
    d_ref[blocks:] = jnp.zeros((SPAN,) + d_ref.shape[1:], BF16)
    some(early, blocks, blocks, lambda places: gate_cotangent(places, g_ref, pre_ref, mixes, d_ref))

    def back(first, count):
        rows = count * row_count
        here = pl.ds(first, count)
        for slab in range(slabs):
            total = g_ref[here, :, cut(slab)].reshape(rows, SLAB).astype(F32)
            for k in range(3):
                later = d_ref[pl.ds(first + k, count), :, cut(slab, 2 * SLAB)].reshape(rows, 2 * SLAB)
                total = total + nt(later, weights[1, slab, cut(k), :])
            between_ref[here, :, cut(slab)] = total.astype(BF16).reshape(count, row_count, SLAB)

    chunks(blocks, back)
    if not early:
        long_conv_sums(blocks, group_size, mid_ref, d_ref, fold, last_ref, slice(0, SLAB))


def own_kernel(x_ref, between_ref, weights, mixes, push_ref, sum_ref):
    row_count, channels = sum_ref.shape
    slabs = channels // SLAB
    z = lax.axis_index("seq") // SPAN
    for j in range(slabs // 2):
        dgated = nt(between_ref[z], mixes[0, cut(j, 2 * SLAB), :])
        for half in range(2):
            slab = j * 2 + half
            taps = [x_ref[z, HALO - k * REACH : HALO - k * REACH + row_count, cut(slab)] for k in range(3)]
            tanh, sig = gates(conv(taps, weights[0, slab]))
            dpre = gate_grad(tanh, sig, dgated[:, cut(half)])
            moved = [nt(dpre, weights[0, slab, cut(k), :]) for k in range(3)]
            first = jnp.concatenate([jnp.zeros((REACH, SLAB), F32), moved[1]], axis=0)
            extended = jnp.concatenate([moved[2], jnp.zeros((HALO, SLAB), F32)], axis=0) + jnp.concatenate(
                [first, jnp.zeros((HALO - REACH, SLAB), F32)], axis=0
            )
            push_ref[:, cut(slab)] = extended[:HALO].astype(BF16)
            sum_ref[:, cut(slab)] = between_ref[z, :, cut(slab)].astype(F32) + moved[0] + extended[HALO:]


def short_kernel(blocks, group_size, x_ref, between_ref, weights, mixes, fold, *refs):
    *long_refs, _, _, own_ref, send_ref, total_ref = refs
    row_count, channels = between_ref.shape[1:]
    pair, wide, first_slab = pair_slabs(channels, blocks)
    rows = blocks * row_count
    between = between_ref[...].reshape(rows, channels)
    for i in range(wide):
        slab = first_slab + i
        taps = [
            x_ref[:blocks, HALO - k * REACH : HALO - k * REACH + row_count, lanes(slab)].reshape(rows, SLAB)
            for k in range(3)
        ]
        tanh, sig = gates(conv(taps, weights[0, slab]))
        dpre = gate_grad(tanh, sig, nt(between, mixes[0, lanes(slab), :]))
        total_ref[cut(i), :channels] = tn((tanh * sig).astype(BF16), between)
        total_ref[cut(i), channels : channels + SLAB] = weight_sums(group_size, taps, dpre, fold[...])
    last = slice(channels + SLAB, channels + 2 * SLAB)
    if len(long_refs) > 1:
        long_conv_sums(blocks, group_size, *long_refs, fold, total_ref, last)
    else:
        total_ref[:, last] = long_refs[0][...]
    split_pair(pair, total_ref, own_ref, send_ref)


def finish_kernel(group_size, mix1, own0, got_mix1, got0, last_cot, other_cot, mix_ref, conv_ref, cot_ref):
    cot_ref[...] = jnp.where(on_last_section(), last_cot[...].astype(F32), other_cot[...].astype(F32)).astype(BF16)
    channels = mix_ref.shape[2]
    width = 2 * group_size
    total = own0[...] + got0[...].astype(F32)
    mix_ref[:, 0, :] = total[:, :channels]
    mix_ref[:, 1, :] = mix1[...] + got_mix1[...].astype(F32)
    for layer in range(2):
        for k in range(3):
            begin = channels + SLAB * layer + width * k
            conv_ref[layer, k] = total[:, begin : begin + width]


def add_kernel(own_ref, pushed_ref, *out_refs):
    rest = own_ref.shape[0] - HALO
    for out_ref in out_refs:
        out_ref[:rest, :] = own_ref[:rest, :].astype(BF16)
        out_ref[rest:, :] = (own_ref[rest:, :] + pushed_ref[...].astype(F32)).astype(BF16)


VMEM = pl.BlockSpec(memory_space=pltpu.VMEM)
ANY = pl.BlockSpec(memory_space=pl.ANY)


def call(resident, kernel, outs, arrays, scratch=(), name=None, aliases={}, far=(), near=True, final=(), us=0.1):
    if resident and near:
        arrays = [a if i in far else pltpu.with_memory_space_constraint(a, pltpu.VMEM) for i, a in enumerate(arrays)]
    make = [jax.ShapeDtypeStruct if i in final or not (resident and near) else pltpu.VMEM for i in range(len(outs))]
    return pl.pallas_call(
        kernel,
        out_shape=[of(shape, kind) for of, (shape, kind) in zip(make, outs)],
        in_specs=[ANY if i in far else VMEM for i in range(len(arrays))],
        out_specs=[VMEM] * len(outs),
        scratch_shapes=[pltpu.VMEM(*s) if isinstance(s, tuple) else s for s in scratch],
        input_output_aliases=aliases,
        compiler_params=pltpu.CompilerParams(vmem_limit_bytes=(24 if resident else 56) * 1024 * 1024),
        cost_estimate=pl.CostEstimate(flops=int(us * SCALE * 1.1e9), bytes_accessed=0, transcendentals=0),
        name=name,
    )(*arrays)


def body(saved_section_input, out_cot, kernel_weight, blend_weight, hazard_head, labels, events):
    first_input, cot = saved_section_input[0], out_cot[0]
    row_count, channels = first_input.shape
    seq = lax.axis_size("seq")
    blocks = seq // SPAN
    groups, group_size = kernel_weight.shape[3:5]
    slabs = channels // SLAB
    share = channels // seq

    ring = [0] + list(range(1, blocks, 2)) + [b for b in range(blocks - 1, 0, -1) if b % 2 == 0]
    hops = list(zip(ring, ring[1:] + ring[:1]))

    def step(value):
        return lax.ppermute(
            value, "seq", [(a * SPAN + y, b * SPAN + y) for a, b in hops for y in range(SPAN)]
        )

    def swap(value):
        return lax.ppermute(value, "seq", [(b, b + 1 - 2 * (b % 2)) for b in range(seq)])

    resident = blocks <= 4
    run = functools.partial(call, resident)

    def relay(copied, *others):
        return run(
            functools.partial(relay_kernel, copied),
            [(a.shape, BF16) for a in others[:copied]] + [((HALO, channels), BF16)],
            list(others),
            [pltpu.SemaphoreType.DMA((max(copied, 1),))],
            name="relay",
            far=range(1, len(others)),
            us=0.3,
        )

    def far(value):
        return pltpu.with_memory_space_constraint(value, pltpu.HBM) if resident else value

    head = far(hazard_head.T)
    tails = [swap(first_input[row_count - HALO :])]
    taps = far(kernel_weight[0].transpose(0, 1, 3, 4, 2).reshape(2, 3, -1, groups))
    mixes, far_cot = far(blend_weight[0]), far(cot)
    sent_rows = row_count + CODE_ROWS
    weights, fold, mixes, head, own_cot = run(
        functools.partial(weight_kernel, group_size),
        [
            ((2, slabs, 3 * SLAB, 2 * SLAB), BF16),
            ((SLAB, 6 * SLAB), BF16),
            (mixes.shape, BF16),
            (head.shape, BF16),
            ((sent_rows, channels), BF16),
        ],
        [taps, mixes, head, far_cot, far(labels[None]), far(events[None])],
        [(taps.shape, BF16)] + [((1, row_count), jnp.int32)] * 2 + [pltpu.SemaphoreType.DMA((6,))],
        name="weights",
        far=range(6),
        us=3.5,
    )
    gated = ((min(blocks, 4) * row_count, channels), BF16)
    x_rows = ((blocks + 1, HALO + row_count, channels), BF16)
    mid_rows = ((blocks + SPAN, row_count, channels), BF16)

    def begin(first, count, values, begun):
        operands = [*values, weights, mixes, *begun]
        return run(
            functools.partial(begin_some, blocks, first, count),
            [x_rows, mid_rows],
            operands,
            [gated, pltpu.SemaphoreType.DMA((count,))],
            name="begin",
            far=range(count),
            aliases={count + 2: 0, count + 3: 1} if begun else {},
            us=0.6 * count,
        )

    begun = []
    inputs, cots = [far(first_input)], [own_cot]
    sent_input = first_input
    for p in range(1, blocks):
        inputs.append(step(sent_input))
        if p == 1:
            sent_input, tail = relay(1, inputs[1], tails[0], fold)
            sent_cot = own_cot
        elif p < blocks - 1:
            sent_input, tail = relay(1, inputs[p])
            if resident and p == blocks - 2:
                begun = begin(0, blocks - 1, inputs, [])
                sent_cot, _ = relay(1, sent_cot, begun[1])
        else:
            (tail,) = relay(0, inputs[p])
        tails.append(swap(tail))
        sent_cot = step(sent_cot)
        cots.append(sent_cot)
    if resident:
        begun = begin(blocks - 1, 1, inputs[-1:], begun)
        inputs = []
    operands = [*inputs, *tails, weights, mixes, head, *begun]
    x, mid, pre, hazard = run(
        functools.partial(forward_kernel, blocks, resident),
        [
            x_rows,
            mid_rows,
            ((blocks, row_count, 2 * channels), BF16),
            ((blocks, head.shape[0], row_count), F32),
        ],
        operands,
        [gated, pltpu.SemaphoreType.DMA((2 * blocks,))],
        name="forward",
        far=range(len(inputs) + blocks),
        aliases={len(operands) - 2: 0, len(operands) - 1: 1} if resident else {},
        us=3,
    )
    wide = max(channels // blocks, SLAB)
    block_rows = ((blocks, row_count, channels), BF16)
    early = blocks - 1 if resident else 0
    d_rows = ((blocks + SPAN, row_count, 2 * channels), BF16)
    codes = ((blocks, CODE_ROWS, row_count), BF16)
    if early:
        g, d, total = run(
            functools.partial(early_kernel, blocks, early),
            [block_rows, d_rows, ((wide, channels), F32)],
            [*cots[:early], pre, hazard, head, mixes],
            [codes, pltpu.SemaphoreType.DMA((2 * early,))],
            name="early",
            far=range(early),
            us=4,
        )
    late = cots[early:]
    g, mine, mix1, send_mix1 = run(
        functools.partial(mix_kernel, blocks, early),
        [block_rows, ((row_count, channels), BF16), ((share, channels), F32), ((share, channels), BF16)],
        [*late, pre, hazard, head] + ([total, g] if early else []),
        [((wide, channels), F32), codes, pltpu.SemaphoreType.DMA((2 * len(late),))],
        name="long_mix",
        aliases={len(late) + 4: 0} if early else {},
        far=range(len(late)),
        us=0.7,
    )
    got_mix1 = swap(send_mix1)
    between, last = run(
        functools.partial(long_kernel, blocks, early, group_size),
        [block_rows, d_rows if early else ((wide, SLAB), F32)],
        [g, mid, pre, weights, mixes, fold] + ([d] if early else []),
        [((8, SLAB), F32) if early else d_rows],
        name="long_backward",
        aliases={6: 1} if early else {},
        us=3.4,
    )
    push, own_sum = run(
        own_kernel,
        [((HALO, channels), BF16), ((row_count, channels), F32)],
        [x, between, weights, mixes],
        name="own_backward",
        us=2.7,
    )
    pushed = lax.ppermute(push, "seq", [(b, b - 1) for b in range(1, seq)])
    sums = channels + 2 * SLAB
    own0, send0 = run(
        functools.partial(short_kernel, blocks, group_size),
        [((share, sums), F32), ((share, sums), BF16)],
        [x, between, weights, mixes, fold] + ([mid, last] if early else [last]) + [push, got_mix1],
        [((wide, sums), F32)],
        name="short_backward",
        far=(7, 8) if early else (6, 7),
        us=8,
    )
    got0 = swap(send0)
    rows_out = ((row_count, channels), BF16)
    input_gradient, sent_gradient = run(add_kernel, [rows_out] * 2, [own_sum, pushed], name="add", final=(0,), us=0.4)
    count = lax.axis_size("section")
    received = lax.ppermute(sent_gradient, "section", [(s, s - 1) for s in range(1, count)])
    mix_share, conv_share, next_cot = run(
        functools.partial(finish_kernel, group_size),
        [((share, 2, channels), F32), ((2, 3, share, 2 * group_size), F32), rows_out],
        [mix1, own0, got_mix1, got0, mine, received],
        name="finish",
        final=(0, 1, 2),
        us=1.4,
    )
    conv_share = conv_share.reshape(2, 3, share // group_size, group_size, 2 * group_size)
    return (input_gradient[None], next_cot[None], mix_share[None], conv_share[None])


def solution(mesh):
    return jax.shard_map(
        body,
        mesh=mesh,
        in_specs=(
            P("section", "seq", None),
            P("section", "seq", None),
            P("section", None, None, None, None, None),
            P("section", None, None, None),
            P(),
            P("seq"),
            P("seq"),
        ),
        out_specs=(
            P("section", "seq", None),
            P("section", "seq", None),
            P("section", "seq", None, None),
            P("section", None, None, "seq", None, None),
        ),
        check_vma=False,
    )
```

```python
import functools

import jax
import jax.numpy as jnp
from jax import lax
from jax.experimental import pallas as pl
from jax.experimental.pallas import tpu as pltpu
from jax.sharding import PartitionSpec as P

SPAN = 2
SLAB = 128
F32 = jnp.float32
BF16 = jnp.bfloat16
HALO = 32
CODE_ROWS = 16
SCALE = 0.5
REACH = 16


def nn(a, b):
    return lax.dot_general(a, b, (((1,), (0,)), ((), ())), preferred_element_type=F32)


def nt(a, b):
    return lax.dot_general(a, b, (((1,), (1,)), ((), ())), preferred_element_type=F32)


def tn(a, b, precision=None):
    return lax.dot_general(a, b, (((0,), (0,)), ((), ())), preferred_element_type=F32, precision=precision)


def sigmoid(x):
    return 0.5 * jnp.tanh(0.5 * x) + 0.5


def lanes(slab, width=SLAB):
    return pl.ds(pl.multiple_of(slab * width, width), width)


def same_group(group_size):
    rows = lax.broadcasted_iota(jnp.int32, (SLAB, 2 * SLAB), 0) // group_size
    columns = lax.broadcasted_iota(jnp.int32, (SLAB, 2 * SLAB), 1) % SLAB // group_size
    return rows == columns


def spread(group_size, shift, width):
    o = lax.broadcasted_iota(jnp.int32, (width, 2 * SLAB), 0) - shift
    column = lax.broadcasted_iota(jnp.int32, (width, 2 * SLAB), 1)
    return (o == column % group_size + jnp.where(column >= SLAB, group_size, 0)).astype(F32)


def conv(taps, weight):
    return nn(jnp.concatenate(taps, axis=1), weight).astype(BF16)


def gates(pre):
    pre = pre.astype(F32)
    return jnp.tanh(pre[:, :SLAB]), sigmoid(pre[:, SLAB:])


def gate_grad(tanh, sig, dgated):
    one = dgated * sig
    return jnp.concatenate(
        [(one * (1.0 - tanh * tanh)).astype(BF16), (one * tanh * (1.0 - sig)).astype(BF16)], axis=1
    )


def cut(slab, width=SLAB):
    return slice(slab * width, (slab + 1) * width)


def chunks(blocks, step):
    some = min(blocks, 4)
    if some == blocks:
        step(0, blocks)
    else:
        pl.loop(0, blocks // some)(lambda i: step(i * some, some))


def ring_place(index, blocks):
    return jnp.where(index <= blocks // 2, jnp.maximum(2 * index - 1, 0), 2 * (blocks - index))


def arrival(p, blocks):
    z = lax.axis_index("seq") // SPAN
    place = jnp.where(z % 2 == 1, (z + 1) // 2, jnp.where(z == 0, 0, blocks - z // 2))
    hops = jnp.where(jnp.asarray(p) % 2 == 1, (p + 1) // 2, blocks - p // 2)
    return ring_place(lax.rem(place - hops + 2 * blocks, blocks), blocks)


def on_last_section():
    return lax.axis_index("section") == lax.axis_size("section") - 1


def start_copies(pairs, sems, first=0):
    copies = [pltpu.make_async_copy(source, target, sems.at[first + i]) for i, (source, target) in enumerate(pairs)]
    for copy in copies:
        copy.start()
    return copies


def finish_copies(copies):
    for copy in copies:
        copy.wait()


def weight_kernel(group_size, far_w, far_mixes, far_head, far_cot, far_labels, far_events, out_ref, fold_ref, mixes_ref,
                  head_ref, cot_ref, w_ref, labels, events, sems):
    row_count = far_cot.shape[0]
    copies = [(far_w, w_ref), (far_labels, labels), (far_events, events), (far_cot, cot_ref.at[pl.ds(0, row_count)])]
    copies = start_copies(copies + [(far_mixes, mixes_ref), (far_head, head_ref)], sems)
    layers, slabs = out_ref.shape[:2]
    width, groups = w_ref.shape[2:]
    rows = slabs * SLAB
    outputs = 2 * group_size
    row = lax.broadcasted_iota(jnp.int32, (rows, groups), 0)
    pick = (row // group_size == lax.broadcasted_iota(jnp.int32, (rows, groups), 1)).astype(F32).astype(BF16)
    row = lax.broadcasted_iota(jnp.int32, (SLAB, width), 0)
    own = lax.broadcasted_iota(jnp.int32, (SLAB, width), 1) // outputs == row % group_size
    o = lax.broadcasted_iota(jnp.int32, (width, 2 * SLAB), 0) % outputs
    column = lax.broadcasted_iota(jnp.int32, (width, 2 * SLAB), 1)
    one_hot = (o == column % group_size + jnp.where(column >= SLAB, group_size, 0)).astype(F32).astype(BF16)
    keep = same_group(group_size)
    cot_ref[row_count:, :] = jnp.zeros((CODE_ROWS, cot_ref.shape[1]), BF16)
    finish_copies(copies[:3])
    code = (labels[...] + head_ref.shape[0] * events[...]).astype(F32)
    cot_ref[row_count:, :row_count] = jnp.broadcast_to(code, (CODE_ROWS, row_count)).astype(BF16)
    for layer in range(layers):
        for k in range(3):
            for slab in range(slabs):
                picked = nt(pick[cut(slab)], w_ref[layer, k])
                tiled = nn(jnp.where(own, picked, 0.0).astype(BF16), one_hot)
                out_ref[layer, slab, cut(k), :] = jnp.where(keep, tiled, 0.0).astype(BF16)
    for k in range(3):
        fold_ref[:, cut(k, 2 * SLAB)] = spread(group_size, outputs * k, SLAB).astype(BF16)
    finish_copies(copies[3:])


def relay_kernel(copied, *refs):
    *copy_refs, tail_ref, sems = refs[-(2 + copied) :]
    copies = start_copies(list(zip(refs[:copied], copy_refs)), sems)
    tail_ref[...] = refs[0][refs[0].shape[0] - HALO :, :]
    finish_copies(copies)


def short_rows(places, begin, end, x_ref, mid_ref, weights, mixes, gated_ref):
    channels, length = x_ref.shape[2], end - begin
    for slab in range(channels // SLAB):
        for i, z in enumerate(places):
            at = [HALO + begin - k * REACH for k in range(3)]
            tanh, sig = gates(conv([x_ref[z, j : j + length, cut(slab)] for j in at], weights[0, slab]))
            gated_ref[cut(i, length), cut(slab)] = (tanh * sig).astype(BF16)
    mixed = nn(gated_ref[: len(places) * length, :], mixes[0])
    for i, z in enumerate(places):
        here = x_ref[z, HALO + begin : HALO + end, :]
        mid_ref[z + SPAN, begin:end, :] = (here.astype(F32) + mixed[cut(i, length)]).astype(BF16)


def begin_kernel(blocks, first, count, inputs, weights, mixes, x_ref, mid_ref, gated_ref, sems):
    row_count = inputs[0].shape[0]
    places = [arrival(first + i, blocks) for i in range(count)]
    copies = start_copies([(a, x_ref.at[z, pl.ds(HALO, row_count)]) for a, z in zip(inputs, places)], sems)
    if first == 0:
        mid_ref[0:SPAN] = jnp.zeros((SPAN,) + mid_ref.shape[1:], BF16)
    finish_copies(copies)
    if count <= 4:
        short_rows(places, HALO, row_count, x_ref, mid_ref, weights, mixes, gated_ref)
    else:
        some(first, first + count, blocks,
             lambda places: short_rows(places, HALO, row_count, x_ref, mid_ref, weights, mixes, gated_ref))


def begin_some(blocks, first, count, *refs):
    x_ref, mid_ref, gated_ref, sems = refs[-4:]
    begin_kernel(blocks, first, count, refs[:count], refs[count], refs[count + 1], x_ref, mid_ref, gated_ref, sems)


def forward_kernel(blocks, resident, *refs):
    inputs, refs = ([], refs) if resident else (refs[:blocks], refs[blocks:])
    tails, refs = refs[:blocks], refs[blocks:]
    weights, mixes, head = refs[:3]
    x_ref, mid_ref, pre_ref, hazard_ref, gated_ref, sems = refs[-6:]
    row_count, channels = mid_ref.shape[1:]
    y = lax.axis_index("seq") % SPAN
    copies = [(tails[p], x_ref.at[arrival(p, blocks) + 1 - y, pl.ds(0, HALO)]) for p in range(blocks)]
    copies = start_copies(copies, sems)
    if not resident:
        late = sems.at[pl.ds(blocks, blocks)]
        begin_kernel(blocks, 0, blocks, inputs, weights, mixes, x_ref, mid_ref, gated_ref, late)

    @pl.when(y == 0)
    def _():
        x_ref[0, :HALO, :] = jnp.zeros((HALO, channels), BF16)

    finish_copies(copies)

    def short(first, count):
        places = [first + i for i in range(count)]
        short_rows(places, 0, HALO, x_ref, mid_ref, weights, mixes, gated_ref)

    chunks(blocks, short)

    def long(first, count):
        for slab in range(channels // SLAB):
            for i in range(count):
                pre = conv([mid_ref[first + i + SPAN - k, :, cut(slab)] for k in range(3)], weights[1, slab])
                pre_ref[first + i, :, cut(slab, 2 * SLAB)] = pre
                tanh, sig = gates(pre)
                gated_ref[cut(i, row_count), cut(slab)] = (tanh * sig).astype(BF16)

        @pl.when(on_last_section())
        def _():
            mixed = nn(gated_ref[...], mixes[1])
            for i in range(count):
                top = (mid_ref[first + i + SPAN].astype(F32) + mixed[cut(i, row_count)]).astype(BF16)
                hazard_ref[first + i] = jax.nn.sigmoid(nt(head[...], top))

    chunks(blocks, long)


def weight_sums(group_size, taps, dpre, fold):
    keep = same_group(group_size)
    product = jnp.concatenate([jnp.where(keep, tn(tap, dpre), 0.0) for tap in taps], axis=1)
    high = product.astype(BF16)
    low = (product - high.astype(F32)).astype(BF16)
    return nt(high, fold) + nt(low, fold)


def pair_slabs(channels, blocks):
    pair = channels // blocks
    return pair, max(pair, SLAB) // SLAB, lax.axis_index("seq") // SPAN * pair // SLAB


def split_pair(pair, total_ref, own_ref, send_ref):
    share = pair // SPAN
    place = lax.axis_index("seq")
    begin = place // SPAN * pair % SLAB if pair < SLAB else 0
    own = pl.multiple_of(begin + place % SPAN * share, share)
    other = pl.multiple_of(begin + (1 - place % SPAN) * share, share)
    own_ref[...] = total_ref[pl.ds(own, share), :]
    send_ref[...] = total_ref[pl.ds(other, share), :].astype(BF16)


def fetch_cotangents(cots, first, blocks, g_ref, code_ref, sems):
    row_count = g_ref.shape[1]
    copies = []
    for i, cot in enumerate(cots):
        z = arrival(first + i, blocks)
        copies.append((cot.at[pl.ds(0, row_count)], g_ref.at[z]))
        copies.append((cot.at[pl.ds(row_count, CODE_ROWS), pl.ds(0, row_count)], code_ref.at[z]))
    return start_copies(copies, sems)


def add_loss(places, code_ref, hazard_ref, head, g_ref):
    @pl.when(on_last_section())
    def _():
        for z in places:
            hazard = hazard_ref[z]
            bins = lax.broadcasted_iota(jnp.int32, hazard.shape, 0).astype(F32)
            code = code_ref[z, 0:1, :].astype(F32)
            event = jnp.where(code >= hazard.shape[0], 1.0, 0.0)
            label = code - hazard.shape[0] * event
            dlogit = jnp.where(bins <= label, hazard, 0.0) - jnp.where(bins == label, event, 0.0)
            g_ref[z] = (g_ref[z].astype(F32) + tn(dlogit.astype(BF16), head[...])).astype(BF16)


def gate_cotangent(places, g_ref, pre_ref, mixes, d_ref):
    rows = g_ref.shape[1]
    g = jnp.concatenate([g_ref[z] for z in places], axis=0)
    for j in range(g_ref.shape[2] // SLAB // 2):
        dgated = nt(g, mixes[1, cut(j, 2 * SLAB), :])
        for half in range(2):
            column = cut(j * 2 + half, 2 * SLAB)
            for i, z in enumerate(places):
                tanh, sig = gates(pre_ref[z, :, column])
                d_ref[z, :, column] = gate_grad(tanh, sig, dgated[cut(i, rows), cut(half)])


def mix_sums(places, g_ref, pre_ref, total_ref):
    channels = g_ref.shape[2]
    _, wide, first_slab = pair_slabs(channels, pre_ref.shape[0])
    g = jnp.concatenate([g_ref[z] for z in places], axis=0)
    for i in range(wide):
        gated = []
        for z in places:
            tanh, sig = gates(pre_ref[z, :, lanes(first_slab + i, 2 * SLAB)])
            gated.append((tanh * sig).astype(BF16))
        total_ref[cut(i), :] += tn(jnp.concatenate(gated, axis=0), g)


def some(first, end, blocks, step):
    if blocks <= 4:
        step([arrival(p, blocks) for p in range(first, end)])
    else:
        pl.loop(first, end)(lambda p: step([arrival(p, blocks)]))


def early_kernel(blocks, early, *refs):
    cots = refs[:early]
    pre_ref, hazard_ref, head, mixes, g_ref, d_ref, total_ref, code_ref, sems = refs[early:]
    copies = fetch_cotangents(cots, 0, blocks, g_ref, code_ref, sems)
    total_ref[...] = jnp.zeros(total_ref.shape, F32)
    finish_copies(copies)

    def one(places):
        add_loss(places, code_ref, hazard_ref, head, g_ref)
        gate_cotangent(places, g_ref, pre_ref, mixes, d_ref)
        mix_sums(places, g_ref, pre_ref, total_ref)

    some(0, early, blocks, one)


def mix_kernel(blocks, early, *refs):
    cots, refs = refs[: blocks - early], refs[blocks - early :]
    pre_ref, hazard_ref, head = refs[:3]
    g_ref, mine_ref, own_ref, send_ref, total_ref, code_ref, sems = refs[-7:]
    copies = fetch_cotangents(cots, early, blocks, g_ref, code_ref, sems)
    total_ref[...] = refs[3][...] if early else jnp.zeros(total_ref.shape, F32)
    finish_copies(copies)

    def one(places):
        add_loss(places, code_ref, hazard_ref, head, g_ref)
        mix_sums(places, g_ref, pre_ref, total_ref)

    some(early, blocks, blocks, one)
    mine_ref[...] = g_ref[lax.axis_index("seq") // SPAN]
    split_pair(g_ref.shape[2] // blocks, total_ref, own_ref, send_ref)


def long_conv_sums(blocks, group_size, mid_ref, d_ref, fold, total_ref, columns, first_slab, wide):
    row_count = mid_ref.shape[1]
    rows = blocks * row_count
    for i in range(wide):
        slab = first_slab + i
        taps = [mid_ref[2 - k : 2 - k + blocks, :, lanes(slab)].reshape(rows, SLAB) for k in range(3)]
        dpre_part = d_ref[:blocks, :, lanes(slab, 2 * SLAB)].reshape(rows, 2 * SLAB)
        total_ref[cut(i), columns] = weight_sums(group_size, taps, dpre_part, fold[...])


def long_kernel(blocks, early, group_size, g_ref, mid_ref, pre_ref, weights, mixes, fold, *refs):
    between_ref, last_ref = refs[-3:-1] if early else refs[:2]
    d_ref = last_ref if early else refs[2]
    row_count, channels = g_ref.shape[1:]
    slabs = channels // SLAB
    d_ref[blocks:] = jnp.zeros((SPAN,) + d_ref.shape[1:], BF16)
    some(early, blocks, blocks, lambda places: gate_cotangent(places, g_ref, pre_ref, mixes, d_ref))

    def back(first, count):
        rows = count * row_count
        here = pl.ds(first, count)
        for slab in range(slabs):
            total = g_ref[here, :, cut(slab)].reshape(rows, SLAB).astype(F32)
            for k in range(3):
                later = d_ref[pl.ds(first + k, count), :, cut(slab, 2 * SLAB)].reshape(rows, 2 * SLAB)
                total = total + nt(later, weights[1, slab, cut(k), :])
            between_ref[here, :, cut(slab)] = total.astype(BF16).reshape(count, row_count, SLAB)

    chunks(blocks, back)
    if not early:
        _, wide, first_slab = pair_slabs(channels, blocks)
        long_conv_sums(blocks, group_size, mid_ref, d_ref, fold, last_ref, slice(0, SLAB), first_slab, wide)


def own_kernel(x_ref, between_ref, weights, mixes, push_ref, sum_ref):
    row_count, channels = sum_ref.shape
    slabs = channels // SLAB
    z = lax.axis_index("seq") // SPAN
    for j in range(slabs // 2):
        dgated = nt(between_ref[z], mixes[0, cut(j, 2 * SLAB), :])
        for half in range(2):
            slab = j * 2 + half
            taps = [x_ref[z, HALO - k * REACH : HALO - k * REACH + row_count, cut(slab)] for k in range(3)]
            tanh, sig = gates(conv(taps, weights[0, slab]))
            dpre = gate_grad(tanh, sig, dgated[:, cut(half)])
            moved = [nt(dpre, weights[0, slab, cut(k), :]) for k in range(3)]
            first = jnp.concatenate([jnp.zeros((REACH, SLAB), F32), moved[1]], axis=0)
            extended = jnp.concatenate([moved[2], jnp.zeros((HALO, SLAB), F32)], axis=0) + jnp.concatenate(
                [first, jnp.zeros((HALO - REACH, SLAB), F32)], axis=0
            )
            push_ref[:, cut(slab)] = extended[:HALO].astype(BF16)
            sum_ref[:, cut(slab)] = between_ref[z, :, cut(slab)].astype(F32) + moved[0] + extended[HALO:]


def short_sums(blocks, group_size, first_slab, wide, x_ref, between_ref, weights, mixes, fold, total_ref):
    row_count, channels = between_ref.shape[1:]
    rows = blocks * row_count
    between = between_ref[...].reshape(rows, channels)
    for i in range(wide):
        slab = first_slab + i
        taps = [
            x_ref[:blocks, HALO - k * REACH : HALO - k * REACH + row_count, lanes(slab)].reshape(rows, SLAB)
            for k in range(3)
        ]
        tanh, sig = gates(conv(taps, weights[0, slab]))
        dpre = gate_grad(tanh, sig, nt(between, mixes[0, lanes(slab), :]))
        total_ref[cut(i), :channels] = tn((tanh * sig).astype(BF16), between)
        total_ref[cut(i), channels : channels + SLAB] = weight_sums(group_size, taps, dpre, fold[...])


def short_kernel(blocks, group_size, x_ref, between_ref, weights, mixes, fold, last, *refs):
    own_ref, send_ref, total_ref = refs[-3:]
    channels = between_ref.shape[2]
    pair, wide, first_slab = pair_slabs(channels, blocks)
    short_sums(blocks, group_size, first_slab, wide, x_ref, between_ref, weights, mixes, fold, total_ref)
    total_ref[:, channels + SLAB :] = last[...]
    split_pair(pair, total_ref, own_ref, send_ref)


def half_kernel(blocks, group_size, partner, x_ref, between_ref, weights, mixes, fold, mid_ref, d_ref, *refs):
    out_ref, total_ref = refs[-2:]
    channels, share = between_ref.shape[2], out_ref.shape[0]
    place = lax.axis_index("seq")
    owner = place + (1 - 2 * (place % SPAN) if partner else 0)
    first_slab, wide = owner * share // SLAB, share // SLAB
    short_sums(blocks, group_size, first_slab, wide, x_ref, between_ref, weights, mixes, fold, total_ref)
    last = slice(channels + SLAB, channels + 2 * SLAB)
    long_conv_sums(blocks, group_size, mid_ref, d_ref, fold, total_ref, last, first_slab, wide)
    out_ref[...] = total_ref[...].astype(out_ref.dtype)


def finish_kernel(group_size, mix1, own0, got_mix1, got0, last_cot, other_cot, mix_ref, conv_ref, cot_ref):
    cot_ref[...] = jnp.where(on_last_section(), last_cot[...].astype(F32), other_cot[...].astype(F32)).astype(BF16)
    channels = mix_ref.shape[2]
    width = 2 * group_size
    total = own0[...] + got0[...].astype(F32)
    mix_ref[:, 0, :] = total[:, :channels]
    mix_ref[:, 1, :] = mix1[...] + got_mix1[...].astype(F32)
    for layer in range(2):
        for k in range(3):
            begin = channels + SLAB * layer + width * k
            conv_ref[layer, k] = total[:, begin : begin + width]


def add_kernel(own_ref, pushed_ref, _, *out_refs):
    rest = own_ref.shape[0] - HALO
    for out_ref in out_refs:
        out_ref[:rest, :] = own_ref[:rest, :].astype(BF16)
        out_ref[rest:, :] = (own_ref[rest:, :] + pushed_ref[...].astype(F32)).astype(BF16)


VMEM = pl.BlockSpec(memory_space=pltpu.VMEM)
ANY = pl.BlockSpec(memory_space=pl.ANY)


def call(resident, kernel, outs, arrays, scratch=(), name=None, aliases={}, far=(), near=True, final=(), us=0.1):
    if resident and near:
        arrays = [a if i in far else pltpu.with_memory_space_constraint(a, pltpu.VMEM) for i, a in enumerate(arrays)]
    make = [jax.ShapeDtypeStruct if i in final or not (resident and near) else pltpu.VMEM for i in range(len(outs))]
    return pl.pallas_call(
        kernel,
        out_shape=[of(shape, kind) for of, (shape, kind) in zip(make, outs)],
        in_specs=[ANY if i in far else VMEM for i in range(len(arrays))],
        out_specs=[VMEM] * len(outs),
        scratch_shapes=[pltpu.VMEM(*s) if isinstance(s, tuple) else s for s in scratch],
        input_output_aliases=aliases,
        compiler_params=pltpu.CompilerParams(vmem_limit_bytes=(24 if resident else 56) * 1024 * 1024),
        cost_estimate=pl.CostEstimate(flops=int(us * SCALE * 1.1e9), bytes_accessed=0, transcendentals=0),
        name=name,
    )(*arrays)


def body(saved_section_input, out_cot, kernel_weight, blend_weight, hazard_head, labels, events):
    first_input, cot = saved_section_input[0], out_cot[0]
    row_count, channels = first_input.shape
    seq = lax.axis_size("seq")
    blocks = seq // SPAN
    groups, group_size = kernel_weight.shape[3:5]
    slabs = channels // SLAB
    share = channels // seq

    ring = [0] + list(range(1, blocks, 2)) + [b for b in range(blocks - 1, 0, -1) if b % 2 == 0]
    hops = list(zip(ring, ring[1:] + ring[:1]))

    def step(value, p):
        pairs = [(a, b) if p % 2 else (b, a) for a, b in hops]
        return lax.ppermute(value, "seq", [(a * SPAN + y, b * SPAN + y) for a, b in pairs for y in range(SPAN)])

    def swap(value):
        return lax.ppermute(value, "seq", [(b, b + 1 - 2 * (b % 2)) for b in range(seq)])

    resident = blocks <= 4
    run = functools.partial(call, resident)

    def relay(copied, *others):
        return run(
            functools.partial(relay_kernel, copied),
            [(a.shape, BF16) for a in others[:copied]] + [((HALO, channels), BF16)],
            list(others),
            [pltpu.SemaphoreType.DMA((max(copied, 1),))],
            name="relay",
            far=range(1, len(others)),
            us=0.3,
        )

    def far(value):
        return pltpu.with_memory_space_constraint(value, pltpu.HBM) if resident else value

    head = far(hazard_head.T)
    tails = [swap(first_input[row_count - HALO :])]
    taps = far(kernel_weight[0].transpose(0, 1, 3, 4, 2).reshape(2, 3, -1, groups))
    mixes, far_cot = far(blend_weight[0]), far(cot)
    sent_rows = row_count + CODE_ROWS
    weights, fold, mixes, head, own_cot = run(
        functools.partial(weight_kernel, group_size),
        [
            ((2, slabs, 3 * SLAB, 2 * SLAB), BF16),
            ((SLAB, 6 * SLAB), BF16),
            (mixes.shape, BF16),
            (head.shape, BF16),
            ((sent_rows, channels), BF16),
        ],
        [taps, mixes, head, far_cot, far(labels[None]), far(events[None])],
        [(taps.shape, BF16)] + [((1, row_count), jnp.int32)] * 2 + [pltpu.SemaphoreType.DMA((6,))],
        name="weights",
        far=range(6),
        us=3.5,
    )
    gated = ((min(blocks, 4) * row_count, channels), BF16)
    x_rows = ((blocks + 1, HALO + row_count, channels), BF16)
    mid_rows = ((blocks + SPAN, row_count, channels), BF16)

    def begin(first, count, values, begun):
        operands = [*values, weights, mixes, *begun]
        return run(
            functools.partial(begin_some, blocks, first, count),
            [x_rows, mid_rows],
            operands,
            [gated, pltpu.SemaphoreType.DMA((count,))],
            name="begin",
            far=range(count),
            aliases={count + 2: 0, count + 3: 1} if begun else {},
            us=0.6 * count,
        )

    begun = []
    inputs, cots = [far(first_input)], [own_cot]
    relayed, sent_cot = [first_input, first_input], own_cot
    for p in range(1, blocks):
        inputs.append(step(relayed[p - 1], p))
        if p == 1:
            sent_input, tail = relay(1, inputs[1], fold)
            relayed.append(sent_input)
        else:
            if p == 2:
                sent_cot, _ = relay(1, own_cot, inputs[p], tails[0])
            (tail,) = relay(0, inputs[p])
            relayed.append(inputs[p])
        tails.append(swap(tail))
    if resident:
        begun = begin(0, blocks - 1, inputs[:-1], [])
        begun = begin(blocks - 1, 1, inputs[-1:], begun)
    relayed = [sent_cot, sent_cot]
    for p in range(1, blocks):
        if p == 2 and resident:
            relayed[1], _ = relay(1, sent_cot, tail)
        cots.append(step(relayed[p - 1], p))
        relayed.append(cots[p])
    if resident:
        inputs = []
    operands = [*inputs, *tails, weights, mixes, head, *begun]
    x, mid, pre, hazard = run(
        functools.partial(forward_kernel, blocks, resident),
        [
            x_rows,
            mid_rows,
            ((blocks, row_count, 2 * channels), BF16),
            ((blocks, head.shape[0], row_count), F32),
        ],
        operands,
        [gated, pltpu.SemaphoreType.DMA((2 * blocks,))],
        name="forward",
        far=range(len(inputs) + blocks),
        aliases={len(operands) - 2: 0, len(operands) - 1: 1} if resident else {},
        us=3,
    )
    wide = max(channels // blocks, SLAB)
    block_rows = ((blocks, row_count, channels), BF16)
    early = blocks - 1 if resident else 0
    d_rows = ((blocks + SPAN, row_count, 2 * channels), BF16)
    codes = ((blocks, CODE_ROWS, row_count), BF16)
    if early:
        g, d, total = run(
            functools.partial(early_kernel, blocks, early),
            [block_rows, d_rows, ((wide, channels), F32)],
            [*cots[:early], pre, hazard, head, mixes],
            [codes, pltpu.SemaphoreType.DMA((2 * early,))],
            name="early",
            far=range(early),
            us=4,
        )
    late = cots[early:]
    g, mine, mix1, send_mix1 = run(
        functools.partial(mix_kernel, blocks, early),
        [block_rows, ((row_count, channels), BF16), ((share, channels), F32), ((share, channels), BF16)],
        [*late, pre, hazard, head] + ([total, g] if early else []),
        [((wide, channels), F32), codes, pltpu.SemaphoreType.DMA((2 * len(late),))],
        name="long_mix",
        aliases={len(late) + 4: 0} if early else {},
        far=range(len(late)),
        us=0.7,
    )
    got_mix1 = swap(send_mix1)
    between, last = run(
        functools.partial(long_kernel, blocks, early, group_size),
        [block_rows, d_rows if early else ((wide, SLAB), F32)],
        [g, mid, pre, weights, mixes, fold] + ([d] if early else []),
        [((8, SLAB), F32) if early else d_rows],
        name="long_backward",
        aliases={6: 1} if early else {},
        us=3.4,
    )
    push, own_sum = run(
        own_kernel,
        [((HALO, channels), BF16), ((row_count, channels), F32)],
        [x, between, weights, mixes],
        name="own_backward",
        us=2.7,
    )
    pushed = lax.ppermute(push, "seq", [(b, b - 1) for b in range(1, seq)])
    sums = channels + 2 * SLAB
    if early:
        half = functools.partial(half_kernel, blocks, group_size)
        held = [x, between, weights, mixes, fold, mid, last]
        (send0,) = run(
            functools.partial(half, True),
            [((share, sums), BF16)],
            [*held, push, got_mix1],
            [((share, sums), F32)],
            name="short_partner",
            far=(7, 8),
            us=4,
        )
    else:
        own0, send0 = run(
            functools.partial(short_kernel, blocks, group_size),
            [((share, sums), F32), ((share, sums), BF16)],
            [x, between, weights, mixes, fold, last],
            [((wide, sums), F32)],
            name="short_backward",
        )
    got0 = swap(send0)
    rows_out = ((row_count, channels), BF16)
    input_gradient, sent_gradient = run(
        add_kernel, [rows_out] * 2, [own_sum, pushed, send0], name="add", final=(0,), far=(2,), us=0.4
    )
    if early:
        (own0,) = run(
            functools.partial(half, False),
            [((share, sums), F32)],
            [*held, sent_gradient],
            [((share, sums), F32)],
            name="short_own",
            far=(7,),
            us=8,
        )
    count = lax.axis_size("section")
    received = lax.ppermute(sent_gradient, "section", [(s, s - 1) for s in range(1, count)])
    mix_share, conv_share, next_cot = run(
        functools.partial(finish_kernel, group_size),
        [((share, 2, channels), F32), ((2, 3, share, 2 * group_size), F32), rows_out],
        [mix1, own0, got_mix1, got0, mine, received],
        name="finish",
        final=(0, 1, 2),
        us=1.4,
    )
    conv_share = conv_share.reshape(2, 3, share // group_size, group_size, 2 * group_size)
    return (input_gradient[None], next_cot[None], mix_share[None], conv_share[None])


def solution(mesh):
    return jax.shard_map(
        body,
        mesh=mesh,
        in_specs=(
            P("section", "seq", None),
            P("section", "seq", None),
            P("section", None, None, None, None, None),
            P("section", None, None, None),
            P(),
            P("seq"),
            P("seq"),
        ),
        out_specs=(
            P("section", "seq", None),
            P("section", "seq", None),
            P("section", "seq", None, None),
            P("section", None, None, "seq", None, None),
        ),
        check_vma=False,
    )
```

```python
import functools

import jax
import jax.numpy as jnp
from jax import lax
from jax.experimental import pallas as pl
from jax.experimental.pallas import tpu as pltpu
from jax.sharding import PartitionSpec as P

SPAN = 2
SLAB = 128
F32 = jnp.float32
BF16 = jnp.bfloat16
HALO = 32
CODE_ROWS = 16
SCALE = 0.5
REACH = 16


def nn(a, b):
    return lax.dot_general(a, b, (((1,), (0,)), ((), ())), preferred_element_type=F32)


def nt(a, b):
    return lax.dot_general(a, b, (((1,), (1,)), ((), ())), preferred_element_type=F32)


def tn(a, b, precision=None):
    return lax.dot_general(a, b, (((0,), (0,)), ((), ())), preferred_element_type=F32, precision=precision)


def sigmoid(x):
    return 0.5 * jnp.tanh(0.5 * x) + 0.5


def lanes(slab, width=SLAB):
    return pl.ds(pl.multiple_of(slab * width, width), width)


def same_group(group_size):
    rows = lax.broadcasted_iota(jnp.int32, (SLAB, 2 * SLAB), 0) // group_size
    columns = lax.broadcasted_iota(jnp.int32, (SLAB, 2 * SLAB), 1) % SLAB // group_size
    return rows == columns


def spread(group_size, shift, width):
    o = lax.broadcasted_iota(jnp.int32, (width, 2 * SLAB), 0) - shift
    column = lax.broadcasted_iota(jnp.int32, (width, 2 * SLAB), 1)
    return (o == column % group_size + jnp.where(column >= SLAB, group_size, 0)).astype(F32)


def conv(taps, weight):
    return nn(jnp.concatenate(taps, axis=1), weight).astype(BF16)


def gates(pre):
    pre = pre.astype(F32)
    return jnp.tanh(pre[:, :SLAB]), sigmoid(pre[:, SLAB:])


def gate_grad(tanh, sig, dgated):
    one = dgated * sig
    return jnp.concatenate(
        [(one * (1.0 - tanh * tanh)).astype(BF16), (one * tanh * (1.0 - sig)).astype(BF16)], axis=1
    )


def cut(slab, width=SLAB):
    return slice(slab * width, (slab + 1) * width)


def chunks(blocks, step):
    some = min(blocks, 4)
    if some == blocks:
        step(0, blocks)
    else:
        pl.loop(0, blocks // some)(lambda i: step(i * some, some))


def ring_place(index, blocks):
    return jnp.where(index <= blocks // 2, jnp.maximum(2 * index - 1, 0), 2 * (blocks - index))


def arrival(p, blocks):
    z = lax.axis_index("seq") // SPAN
    place = jnp.where(z % 2 == 1, (z + 1) // 2, jnp.where(z == 0, 0, blocks - z // 2))
    hops = jnp.where(jnp.asarray(p) % 2 == 1, (p + 1) // 2, blocks - p // 2)
    return ring_place(lax.rem(place - hops + 2 * blocks, blocks), blocks)


def on_last_section():
    return lax.axis_index("section") == lax.axis_size("section") - 1


def start_copies(pairs, sems, first=0):
    copies = [pltpu.make_async_copy(source, target, sems.at[first + i]) for i, (source, target) in enumerate(pairs)]
    for copy in copies:
        copy.start()
    return copies


def finish_copies(copies):
    for copy in copies:
        copy.wait()


def weight_kernel(group_size, far_w, far_mixes, far_head, far_cot, far_labels, far_events, out_ref, fold_ref, mixes_ref,
                  head_ref, cot_ref, w_ref, labels, events, sems):
    row_count = far_cot.shape[0]
    copies = [(far_w, w_ref), (far_labels, labels), (far_events, events), (far_cot, cot_ref.at[pl.ds(0, row_count)])]
    copies = start_copies(copies + [(far_mixes, mixes_ref), (far_head, head_ref)], sems)
    layers, slabs = out_ref.shape[:2]
    width, groups = w_ref.shape[2:]
    rows = slabs * SLAB
    outputs = 2 * group_size
    row = lax.broadcasted_iota(jnp.int32, (rows, groups), 0)
    pick = (row // group_size == lax.broadcasted_iota(jnp.int32, (rows, groups), 1)).astype(F32).astype(BF16)
    row = lax.broadcasted_iota(jnp.int32, (SLAB, width), 0)
    own = lax.broadcasted_iota(jnp.int32, (SLAB, width), 1) // outputs == row % group_size
    o = lax.broadcasted_iota(jnp.int32, (width, 2 * SLAB), 0) % outputs
    column = lax.broadcasted_iota(jnp.int32, (width, 2 * SLAB), 1)
    one_hot = (o == column % group_size + jnp.where(column >= SLAB, group_size, 0)).astype(F32).astype(BF16)
    keep = same_group(group_size)
    cot_ref[row_count:, :] = jnp.zeros((CODE_ROWS, cot_ref.shape[1]), BF16)
    finish_copies(copies[:3])
    code = (labels[...] + head_ref.shape[0] * events[...]).astype(F32)
    cot_ref[row_count:, :row_count] = jnp.broadcast_to(code, (CODE_ROWS, row_count)).astype(BF16)
    for layer in range(layers):
        for k in range(3):
            for slab in range(slabs):
                picked = nt(pick[cut(slab)], w_ref[layer, k])
                tiled = nn(jnp.where(own, picked, 0.0).astype(BF16), one_hot)
                out_ref[layer, slab, cut(k), :] = jnp.where(keep, tiled, 0.0).astype(BF16)
    for k in range(3):
        fold_ref[:, cut(k, 2 * SLAB)] = spread(group_size, outputs * k, SLAB).astype(BF16)
    finish_copies(copies[3:])


def relay_kernel(copied, *refs):
    *copy_refs, tail_ref, sems = refs[-(2 + copied) :]
    copies = start_copies(list(zip(refs[:copied], copy_refs)), sems)
    tail_ref[...] = refs[0][refs[0].shape[0] - HALO :, :]
    finish_copies(copies)


def short_rows(places, begin, end, x_ref, mid_ref, weights, mixes, gated_ref):
    channels, length = x_ref.shape[2], end - begin
    for slab in range(channels // SLAB):
        for i, z in enumerate(places):
            at = [HALO + begin - k * REACH for k in range(3)]
            tanh, sig = gates(conv([x_ref[z, j : j + length, cut(slab)] for j in at], weights[0, slab]))
            gated_ref[cut(i, length), cut(slab)] = (tanh * sig).astype(BF16)
    mixed = nn(gated_ref[: len(places) * length, :], mixes[0])
    for i, z in enumerate(places):
        here = x_ref[z, HALO + begin : HALO + end, :]
        mid_ref[z + SPAN, begin:end, :] = (here.astype(F32) + mixed[cut(i, length)]).astype(BF16)


def begin_kernel(blocks, first, count, inputs, weights, mixes, x_ref, mid_ref, gated_ref, sems):
    row_count = inputs[0].shape[0]
    places = [arrival(first + i, blocks) for i in range(count)]
    copies = start_copies([(a, x_ref.at[z, pl.ds(HALO, row_count)]) for a, z in zip(inputs, places)], sems)
    if first == 0:
        mid_ref[0:SPAN] = jnp.zeros((SPAN,) + mid_ref.shape[1:], BF16)
    finish_copies(copies)
    if count <= 4:
        short_rows(places, HALO, row_count, x_ref, mid_ref, weights, mixes, gated_ref)
    else:
        some(first, first + count, blocks,
             lambda places: short_rows(places, HALO, row_count, x_ref, mid_ref, weights, mixes, gated_ref))


def begin_some(blocks, first, count, *refs):
    x_ref, mid_ref, gated_ref, sems = refs[-4:]
    begin_kernel(blocks, first, count, refs[:count], refs[count], refs[count + 1], x_ref, mid_ref, gated_ref, sems)


def forward_kernel(blocks, resident, *refs):
    inputs, refs = ([], refs) if resident else (refs[:blocks], refs[blocks:])
    tails, refs = refs[:blocks], refs[blocks:]
    weights, mixes, head = refs[:3]
    x_ref, mid_ref, pre_ref, hazard_ref, gated_ref, sems = refs[-6:]
    row_count, channels = mid_ref.shape[1:]
    y = lax.axis_index("seq") % SPAN
    copies = [(tails[p], x_ref.at[arrival(p, blocks) + 1 - y, pl.ds(0, HALO)]) for p in range(blocks)]
    copies = start_copies(copies, sems)
    if not resident:
        late = sems.at[pl.ds(blocks, blocks)]
        begin_kernel(blocks, 0, blocks, inputs, weights, mixes, x_ref, mid_ref, gated_ref, late)

    @pl.when(y == 0)
    def _():
        x_ref[0, :HALO, :] = jnp.zeros((HALO, channels), BF16)

    finish_copies(copies)

    def short(first, count):
        places = [first + i for i in range(count)]
        short_rows(places, 0, HALO, x_ref, mid_ref, weights, mixes, gated_ref)

    chunks(blocks, short)

    def long(first, count):
        for slab in range(channels // SLAB):
            for i in range(count):
                pre = conv([mid_ref[first + i + SPAN - k, :, cut(slab)] for k in range(3)], weights[1, slab])
                pre_ref[first + i, :, cut(slab, 2 * SLAB)] = pre
                tanh, sig = gates(pre)
                gated_ref[cut(i, row_count), cut(slab)] = (tanh * sig).astype(BF16)

        @pl.when(on_last_section())
        def _():
            mixed = nn(gated_ref[...], mixes[1])
            for i in range(count):
                top = (mid_ref[first + i + SPAN].astype(F32) + mixed[cut(i, row_count)]).astype(BF16)
                hazard_ref[first + i] = jax.nn.sigmoid(nt(head[...], top))

    chunks(blocks, long)


def weight_sums(group_size, taps, dpre, fold):
    keep = same_group(group_size)
    product = jnp.concatenate([jnp.where(keep, tn(tap, dpre), 0.0) for tap in taps], axis=1)
    high = product.astype(BF16)
    low = (product - high.astype(F32)).astype(BF16)
    return nt(high, fold) + nt(low, fold)


def pair_slabs(channels, blocks):
    pair = channels // blocks
    return pair, max(pair, SLAB) // SLAB, lax.axis_index("seq") // SPAN * pair // SLAB


def split_pair(pair, total_ref, own_ref, send_ref):
    share = pair // SPAN
    place = lax.axis_index("seq")
    begin = place // SPAN * pair % SLAB if pair < SLAB else 0
    own = pl.multiple_of(begin + place % SPAN * share, share)
    other = pl.multiple_of(begin + (1 - place % SPAN) * share, share)
    own_ref[...] = total_ref[pl.ds(own, share), :]
    send_ref[...] = total_ref[pl.ds(other, share), :].astype(BF16)


def fetch_cotangents(cots, first, blocks, g_ref, code_ref, sems):
    row_count = g_ref.shape[1]
    copies = []
    for i, cot in enumerate(cots):
        z = arrival(first + i, blocks)
        copies.append((cot.at[pl.ds(0, row_count)], g_ref.at[z]))
        copies.append((cot.at[pl.ds(row_count, CODE_ROWS), pl.ds(0, row_count)], code_ref.at[z]))
    return start_copies(copies, sems)


def add_loss(places, code_ref, hazard_ref, head, g_ref):
    @pl.when(on_last_section())
    def _():
        for z in places:
            hazard = hazard_ref[z]
            bins = lax.broadcasted_iota(jnp.int32, hazard.shape, 0).astype(F32)
            code = code_ref[z, 0:1, :].astype(F32)
            event = jnp.where(code >= hazard.shape[0], 1.0, 0.0)
            label = code - hazard.shape[0] * event
            dlogit = jnp.where(bins <= label, hazard, 0.0) - jnp.where(bins == label, event, 0.0)
            g_ref[z] = (g_ref[z].astype(F32) + tn(dlogit.astype(BF16), head[...])).astype(BF16)


def gate_cotangent(places, g_ref, pre_ref, mixes, d_ref):
    rows = g_ref.shape[1]
    g = jnp.concatenate([g_ref[z] for z in places], axis=0)
    for j in range(g_ref.shape[2] // SLAB // 2):
        dgated = nt(g, mixes[1, cut(j, 2 * SLAB), :])
        for half in range(2):
            column = cut(j * 2 + half, 2 * SLAB)
            for i, z in enumerate(places):
                tanh, sig = gates(pre_ref[z, :, column])
                d_ref[z, :, column] = gate_grad(tanh, sig, dgated[cut(i, rows), cut(half)])


def mix_sums(places, g_ref, pre_ref, total_ref):
    channels = g_ref.shape[2]
    _, wide, first_slab = pair_slabs(channels, pre_ref.shape[0])
    g = jnp.concatenate([g_ref[z] for z in places], axis=0)
    for i in range(wide):
        gated = []
        for z in places:
            tanh, sig = gates(pre_ref[z, :, lanes(first_slab + i, 2 * SLAB)])
            gated.append((tanh * sig).astype(BF16))
        total_ref[cut(i), :channels] += tn(jnp.concatenate(gated, axis=0), g)


def some(first, end, blocks, step):
    if blocks <= 4:
        step([arrival(p, blocks) for p in range(first, end)])
    else:
        pl.loop(first, end)(lambda p: step([arrival(p, blocks)]))


def early_kernel(blocks, early, *refs):
    cots = refs[:early]
    pre_ref, hazard_ref, head, mixes, g_ref, d_ref, total_ref, code_ref, sems = refs[early:]
    copies = fetch_cotangents(cots, 0, blocks, g_ref, code_ref, sems)
    d_ref[blocks:] = jnp.zeros((SPAN,) + d_ref.shape[1:], BF16)
    total_ref[...] = jnp.zeros(total_ref.shape, F32)
    finish_copies(copies)

    def one(places):
        add_loss(places, code_ref, hazard_ref, head, g_ref)
        gate_cotangent(places, g_ref, pre_ref, mixes, d_ref)
        mix_sums(places, g_ref, pre_ref, total_ref)

    some(0, early, blocks, one)


def mix_kernel(blocks, early, group_size, *refs):
    cots, refs = refs[: blocks - early], refs[blocks - early :]
    pre_ref, hazard_ref, head = refs[:3]
    mine_ref, own_ref, send_ref, total_ref, code_ref, sems = refs[-6:]
    g_ref = refs[-8] if early else refs[-7]
    copies = fetch_cotangents(cots, early, blocks, g_ref, code_ref, sems)
    channels = g_ref.shape[2]
    if early:
        total_ref[:, :channels] = refs[3][...]
        mid_ref, mixes, fold, d_ref = refs[6], refs[7], refs[8], refs[-7]
    else:
        total_ref[...] = jnp.zeros(total_ref.shape, F32)
    finish_copies(copies)

    def one(places):
        add_loss(places, code_ref, hazard_ref, head, g_ref)
        if early:
            gate_cotangent(places, g_ref, pre_ref, mixes, d_ref)
        mix_sums(places, g_ref, pre_ref, total_ref)

    some(early, blocks, blocks, one)
    if early:
        _, wide, first_slab = pair_slabs(channels, blocks)
        last = slice(channels, channels + SLAB)
        long_conv_sums(blocks, group_size, mid_ref, d_ref, fold, total_ref, last, first_slab, wide)
    mine_ref[...] = g_ref[lax.axis_index("seq") // SPAN]
    split_pair(g_ref.shape[2] // blocks, total_ref, own_ref, send_ref)


def long_conv_sums(blocks, group_size, mid_ref, d_ref, fold, total_ref, columns, first_slab, wide):
    row_count = mid_ref.shape[1]
    rows = blocks * row_count
    for i in range(wide):
        slab = first_slab + i
        taps = [mid_ref[2 - k : 2 - k + blocks, :, lanes(slab)].reshape(rows, SLAB) for k in range(3)]
        dpre_part = d_ref[:blocks, :, lanes(slab, 2 * SLAB)].reshape(rows, 2 * SLAB)
        total_ref[cut(i), columns] = weight_sums(group_size, taps, dpre_part, fold[...])


def long_kernel(blocks, early, group_size, g_ref, mid_ref, pre_ref, weights, mixes, fold, *refs):
    if early:
        d_ref, between_ref = refs
    else:
        between_ref, last_ref, d_ref = refs
    row_count, channels = g_ref.shape[1:]
    slabs = channels // SLAB
    if not early:
        d_ref[blocks:] = jnp.zeros((SPAN,) + d_ref.shape[1:], BF16)
        some(0, blocks, blocks, lambda places: gate_cotangent(places, g_ref, pre_ref, mixes, d_ref))

    def back(first, count):
        rows = count * row_count
        here = pl.ds(first, count)
        for slab in range(slabs):
            total = g_ref[here, :, cut(slab)].reshape(rows, SLAB).astype(F32)
            for k in range(3):
                later = d_ref[pl.ds(first + k, count), :, cut(slab, 2 * SLAB)].reshape(rows, 2 * SLAB)
                total = total + nt(later, weights[1, slab, cut(k), :])
            between_ref[here, :, cut(slab)] = total.astype(BF16).reshape(count, row_count, SLAB)

    chunks(blocks, back)
    if not early:
        _, wide, first_slab = pair_slabs(channels, blocks)
        long_conv_sums(blocks, group_size, mid_ref, d_ref, fold, last_ref, slice(0, SLAB), first_slab, wide)


def own_kernel(x_ref, between_ref, weights, mixes, push_ref, sum_ref):
    row_count, channels = sum_ref.shape
    slabs = channels // SLAB
    z = lax.axis_index("seq") // SPAN
    for j in range(slabs // 2):
        dgated = nt(between_ref[z], mixes[0, cut(j, 2 * SLAB), :])
        for half in range(2):
            slab = j * 2 + half
            taps = [x_ref[z, HALO - k * REACH : HALO - k * REACH + row_count, cut(slab)] for k in range(3)]
            tanh, sig = gates(conv(taps, weights[0, slab]))
            dpre = gate_grad(tanh, sig, dgated[:, cut(half)])
            moved = [nt(dpre, weights[0, slab, cut(k), :]) for k in range(3)]
            first = jnp.concatenate([jnp.zeros((REACH, SLAB), F32), moved[1]], axis=0)
            extended = jnp.concatenate([moved[2], jnp.zeros((HALO, SLAB), F32)], axis=0) + jnp.concatenate(
                [first, jnp.zeros((HALO - REACH, SLAB), F32)], axis=0
            )
            push_ref[:, cut(slab)] = extended[:HALO].astype(BF16)
            sum_ref[:, cut(slab)] = between_ref[z, :, cut(slab)].astype(F32) + moved[0] + extended[HALO:]


def short_sums(blocks, group_size, first_slab, wide, x_ref, between_ref, weights, mixes, fold, total_ref):
    row_count, channels = between_ref.shape[1:]
    rows = blocks * row_count
    between = between_ref[...].reshape(rows, channels)
    for i in range(wide):
        slab = first_slab + i
        taps = [
            x_ref[:blocks, HALO - k * REACH : HALO - k * REACH + row_count, lanes(slab)].reshape(rows, SLAB)
            for k in range(3)
        ]
        tanh, sig = gates(conv(taps, weights[0, slab]))
        dpre = gate_grad(tanh, sig, nt(between, mixes[0, lanes(slab), :]))
        total_ref[cut(i), :channels] = tn((tanh * sig).astype(BF16), between)
        total_ref[cut(i), channels : channels + SLAB] = weight_sums(group_size, taps, dpre, fold[...])


def short_kernel(blocks, group_size, x_ref, between_ref, weights, mixes, fold, last, *refs):
    own_ref, send_ref, total_ref = refs[-3:]
    channels = between_ref.shape[2]
    pair, wide, first_slab = pair_slabs(channels, blocks)
    short_sums(blocks, group_size, first_slab, wide, x_ref, between_ref, weights, mixes, fold, total_ref)
    total_ref[:, channels + SLAB :] = last[...]
    split_pair(pair, total_ref, own_ref, send_ref)


def half_kernel(blocks, group_size, partner, x_ref, between_ref, weights, mixes, fold, *refs):
    out_ref, total_ref = refs[-2:]
    channels, share = between_ref.shape[2], out_ref.shape[0]
    place = lax.axis_index("seq")
    owner = place + (1 - 2 * (place % SPAN) if partner else 0)
    first_slab, wide = owner * share // SLAB, share // SLAB
    short_sums(blocks, group_size, first_slab, wide, x_ref, between_ref, weights, mixes, fold, total_ref)
    out_ref[...] = total_ref[...].astype(out_ref.dtype)


def finish_kernel(group_size, mix1, own0, got_mix1, got0, last_cot, other_cot, mix_ref, conv_ref, cot_ref):
    cot_ref[...] = jnp.where(on_last_section(), last_cot[...].astype(F32), other_cot[...].astype(F32)).astype(BF16)
    channels = mix_ref.shape[2]
    width = 2 * group_size
    total = own0[...] + got0[...].astype(F32)
    mix_ref[:, 0, :] = total[:, :channels]
    total1 = mix1[...] + got_mix1[...].astype(F32)
    mix_ref[:, 1, :] = total1[:, :channels]
    convs = (total[:, channels:], total1[:, channels:] if total1.shape[1] > channels else total[:, channels + SLAB :])
    for layer in range(2):
        for k in range(3):
            conv_ref[layer, k] = convs[layer][:, width * k : width * (k + 1)]


def add_kernel(own_ref, pushed_ref, _, *out_refs):
    rest = own_ref.shape[0] - HALO
    for out_ref in out_refs:
        out_ref[:rest, :] = own_ref[:rest, :].astype(BF16)
        out_ref[rest:, :] = (own_ref[rest:, :] + pushed_ref[...].astype(F32)).astype(BF16)


VMEM = pl.BlockSpec(memory_space=pltpu.VMEM)
ANY = pl.BlockSpec(memory_space=pl.ANY)


def call(resident, kernel, outs, arrays, scratch=(), name=None, aliases={}, far=(), near=True, final=(), us=0.1):
    if resident and near:
        arrays = [a if i in far else pltpu.with_memory_space_constraint(a, pltpu.VMEM) for i, a in enumerate(arrays)]
    make = [jax.ShapeDtypeStruct if i in final or not (resident and near) else pltpu.VMEM for i in range(len(outs))]
    return pl.pallas_call(
        kernel,
        out_shape=[of(shape, kind) for of, (shape, kind) in zip(make, outs)],
        in_specs=[ANY if i in far else VMEM for i in range(len(arrays))],
        out_specs=[VMEM] * len(outs),
        scratch_shapes=[pltpu.VMEM(*s) if isinstance(s, tuple) else s for s in scratch],
        input_output_aliases=aliases,
        compiler_params=pltpu.CompilerParams(vmem_limit_bytes=(24 if resident else 56) * 1024 * 1024),
        cost_estimate=pl.CostEstimate(flops=int(us * SCALE * 1.1e9), bytes_accessed=0, transcendentals=0),
        name=name,
    )(*arrays)


def body(saved_section_input, out_cot, kernel_weight, blend_weight, hazard_head, labels, events):
    first_input, cot = saved_section_input[0], out_cot[0]
    row_count, channels = first_input.shape
    seq = lax.axis_size("seq")
    blocks = seq // SPAN
    groups, group_size = kernel_weight.shape[3:5]
    slabs = channels // SLAB
    share = channels // seq

    ring = [0] + list(range(1, blocks, 2)) + [b for b in range(blocks - 1, 0, -1) if b % 2 == 0]
    hops = list(zip(ring, ring[1:] + ring[:1]))

    def step(value, p):
        pairs = [(a, b) if p % 2 else (b, a) for a, b in hops]
        return lax.ppermute(value, "seq", [(a * SPAN + y, b * SPAN + y) for a, b in pairs for y in range(SPAN)])

    def swap(value):
        return lax.ppermute(value, "seq", [(b, b + 1 - 2 * (b % 2)) for b in range(seq)])

    resident = blocks <= 4
    run = functools.partial(call, resident)

    def relay(copied, *others):
        return run(
            functools.partial(relay_kernel, copied),
            [(a.shape, BF16) for a in others[:copied]] + [((HALO, channels), BF16)],
            list(others),
            [pltpu.SemaphoreType.DMA((max(copied, 1),))],
            name="relay",
            far=range(1, len(others)),
            us=0.3,
        )

    def far(value):
        return pltpu.with_memory_space_constraint(value, pltpu.HBM) if resident else value

    head = far(hazard_head.T)
    tails = [swap(first_input[row_count - HALO :])]
    taps = far(kernel_weight[0].transpose(0, 1, 3, 4, 2).reshape(2, 3, -1, groups))
    mixes, far_cot = far(blend_weight[0]), far(cot)
    sent_rows = row_count + CODE_ROWS
    weights, fold, mixes, head, own_cot = run(
        functools.partial(weight_kernel, group_size),
        [
            ((2, slabs, 3 * SLAB, 2 * SLAB), BF16),
            ((SLAB, 6 * SLAB), BF16),
            (mixes.shape, BF16),
            (head.shape, BF16),
            ((sent_rows, channels), BF16),
        ],
        [taps, mixes, head, far_cot, far(labels[None]), far(events[None])],
        [(taps.shape, BF16)] + [((1, row_count), jnp.int32)] * 2 + [pltpu.SemaphoreType.DMA((6,))],
        name="weights",
        far=range(6),
        us=3.5,
    )
    gated = ((min(blocks, 4) * row_count, channels), BF16)
    x_rows = ((blocks + 1, HALO + row_count, channels), BF16)
    mid_rows = ((blocks + SPAN, row_count, channels), BF16)

    def begin(first, count, values, begun):
        operands = [*values, weights, mixes, *begun]
        return run(
            functools.partial(begin_some, blocks, first, count),
            [x_rows, mid_rows],
            operands,
            [gated, pltpu.SemaphoreType.DMA((count,))],
            name="begin",
            far=range(count),
            aliases={count + 2: 0, count + 3: 1} if begun else {},
            us=0.6 * count,
        )

    begun = []
    inputs, cots = [far(first_input)], [own_cot]
    relayed, sent_cot = [first_input, first_input], own_cot
    for p in range(1, blocks):
        inputs.append(step(relayed[p - 1], p))
        if p == 1:
            sent_input, tail = relay(1, inputs[1], fold)
            relayed.append(sent_input)
        else:
            if p == 2:
                sent_cot, _ = relay(1, own_cot, inputs[p], tails[0])
            (tail,) = relay(0, inputs[p])
            relayed.append(inputs[p])
        tails.append(swap(tail))
    if resident:
        begun = begin(0, blocks - 1, inputs[:-1], [])
        begun = begin(blocks - 1, 1, inputs[-1:], begun)
    relayed = [sent_cot, sent_cot]
    for p in range(1, blocks):
        if p == 2 and resident:
            relayed[1], _ = relay(1, sent_cot, tail)
        cots.append(step(relayed[p - 1], p))
        relayed.append(cots[p])
    if resident:
        inputs = []
    operands = [*inputs, *tails, weights, mixes, head, *begun]
    x, mid, pre, hazard = run(
        functools.partial(forward_kernel, blocks, resident),
        [
            x_rows,
            mid_rows,
            ((blocks, row_count, 2 * channels), BF16),
            ((blocks, head.shape[0], row_count), F32),
        ],
        operands,
        [gated, pltpu.SemaphoreType.DMA((2 * blocks,))],
        name="forward",
        far=range(len(inputs) + blocks),
        aliases={len(operands) - 2: 0, len(operands) - 1: 1} if resident else {},
        us=3,
    )
    wide = max(channels // blocks, SLAB)
    block_rows = ((blocks, row_count, channels), BF16)
    early = blocks - 1 if resident else 0
    d_rows = ((blocks + SPAN, row_count, 2 * channels), BF16)
    codes = ((blocks, CODE_ROWS, row_count), BF16)
    if early:
        g, d, total = run(
            functools.partial(early_kernel, blocks, early),
            [block_rows, d_rows, ((wide, channels), F32)],
            [*cots[:early], pre, hazard, head, mixes],
            [codes, pltpu.SemaphoreType.DMA((2 * early,))],
            name="early",
            far=range(early),
            us=4,
        )
    late = cots[early:]
    sums1 = channels + SLAB * bool(early)
    g, *d_out, mine, mix1, send_mix1 = run(
        functools.partial(mix_kernel, blocks, early, group_size),
        [block_rows]
        + [d_rows] * bool(early)
        + [((row_count, channels), BF16), ((share, sums1), F32), ((share, sums1), BF16)],
        [*late, pre, hazard, head] + ([total, g, d, mid, mixes, fold] if early else []),
        [((wide, sums1), F32), codes, pltpu.SemaphoreType.DMA((2 * len(late),))],
        name="long_mix",
        aliases={len(late) + 4: 0, len(late) + 5: 1} if early else {},
        far=range(len(late)),
        us=1.7,
    )
    got_mix1 = swap(send_mix1)
    between, *last = run(
        functools.partial(long_kernel, blocks, early, group_size),
        [block_rows] + ([] if early else [((wide, SLAB), F32)]),
        [g, mid, pre, weights, mixes, fold, *d_out],
        [] if early else [d_rows],
        name="long_backward",
        us=2,
    )
    push, own_sum = run(
        own_kernel,
        [((HALO, channels), BF16), ((row_count, channels), F32)],
        [x, between, weights, mixes],
        name="own_backward",
        us=2.7,
    )
    pushed = lax.ppermute(push, "seq", [(b, b - 1) for b in range(1, seq)])
    sums = channels + SLAB * (1 if early else 2)
    if early:
        half = functools.partial(half_kernel, blocks, group_size)
        held = [x, between, weights, mixes, fold]
        (send0,) = run(
            functools.partial(half, True),
            [((share, sums), BF16)],
            [*held, push, got_mix1],
            [((share, sums), F32)],
            name="short_partner",
            far=(5, 6),
            us=4,
        )
    else:
        own0, send0 = run(
            functools.partial(short_kernel, blocks, group_size),
            [((share, sums), F32), ((share, sums), BF16)],
            [x, between, weights, mixes, fold, *last],
            [((wide, sums), F32)],
            name="short_backward",
        )
    got0 = swap(send0)
    rows_out = ((row_count, channels), BF16)
    input_gradient, sent_gradient = run(
        add_kernel, [rows_out] * 2, [own_sum, pushed, send0], name="add", final=(0,), far=(2,), us=0.4
    )
    if early:
        (own0,) = run(
            functools.partial(half, False),
            [((share, sums), F32)],
            [*held, sent_gradient],
            [((share, sums), F32)],
            name="short_own",
            far=(5,),
            us=8,
        )
    count = lax.axis_size("section")
    received = lax.ppermute(sent_gradient, "section", [(s, s - 1) for s in range(1, count)])
    mix_share, conv_share, next_cot = run(
        functools.partial(finish_kernel, group_size),
        [((share, 2, channels), F32), ((2, 3, share, 2 * group_size), F32), rows_out],
        [mix1, own0, got_mix1, got0, mine, received],
        name="finish",
        final=(0, 1, 2),
        us=1.4,
    )
    conv_share = conv_share.reshape(2, 3, share // group_size, group_size, 2 * group_size)
    return (input_gradient[None], next_cot[None], mix_share[None], conv_share[None])


def solution(mesh):
    return jax.shard_map(
        body,
        mesh=mesh,
        in_specs=(
            P("section", "seq", None),
            P("section", "seq", None),
            P("section", None, None, None, None, None),
            P("section", None, None, None),
            P(),
            P("seq"),
            P("seq"),
        ),
        out_specs=(
            P("section", "seq", None),
            P("section", "seq", None),
            P("section", "seq", None, None),
            P("section", None, None, "seq", None, None),
        ),
        check_vma=False,
    )
```
